32 devices in a mesh: graph: 16 (over z, x, core), basis: 2 (over y).
Axes of the slice: x: 2, y: 2, z: 4, core: 2. Of those that a mesh axis runs over, the one named last changes fastest.
Arguments:
- edge_feats: bfloat16 [16384, 512], P(('graph', 'basis')), may hold values from -6 to 6
- pre_weight: bfloat16 [512, 512], replicated, may hold values from -0.25 to 0.25
- down_weight: bfloat16 [512, 64], replicated, may hold values from -0.25 to 0.25
- angle_tiles: bfloat16 [384, 2, 128, 128], P('graph', 'basis'), may hold values from -0.5 to 0.5
- part_source: int32 [384], P('graph'), may hold values from 0 to 7
- part_owner: int32 [384, 1], P('graph'), may hold values from 0 to 15; in each aligned block of 24 rows (0 to 23, 24 to 47, ...) at most 3 rows name the same one
- part_target: int32 [384], P('graph'), may hold values from 0 to 7
- up_weight: bfloat16 [2, 64, 512], P('basis'), may hold values from -0.5 to 0.5
- res_first: bfloat16 [512, 512], replicated, may hold values from -0.25 to 0.25
- res_second: bfloat16 [512, 512], replicated, may hold values from -0.25 to 0.25
- edge_slot: int32 [32, 512], P(('graph', 'basis')), may hold values from 0 to 127, never falling along the last dimension, each value on 1 to 8 neighbouring positions
- slot_owner: int32 [32, 128, 1], P(('graph', 'basis')), may hold values from 0 to 15; in each aligned block of 128 rows (0 to 127, 128 to 255, ..., all dimensions but the last counted through in order) at most 16 rows name the same one
- slot_atom: int32 [32, 128], P(('graph', 'basis')), may hold values from 0 to 31
- atom_feats: bfloat16 [1024, 512], P(('graph', 'basis')), may hold values from -6 to 6
- atom_first: bfloat16 [512, 512], replicated, may hold values from -0.25 to 0.25
- atom_second: bfloat16 [512, 512], replicated, may hold values from -0.25 to 0.25
Outputs:
- edge_update: bfloat16 [16384, 512], P(('graph', 'basis'))
- atom_update: bfloat16 [1024, 512], P(('graph', 'basis'))
The draws below stay inside these ranges and needn't reach their ends.
Inputs may be any that keep to these rules, and one draw needn't show every extreme that they name: `part_owner`: the 24 parts of one graph shard name each shard at most 3 times, a bound that some block reaches. `slot_owner`: the 128 slots of one device name each graph shard at most 16 times, a bound that some block reaches. `edge_slot`: along a device's 512 rows the slot never falls; every slot holds 1 to 8 rows, one exactly 8.
All inputs are finite; a program needn't handle non-finite values.
Results may differ from the reference program's by a relative error of at most 0.015.
Values may be sent and summed in bfloat16 or wider, within the bound.
A program may use at most 64 MiB of HBM per device.

```python
import math
import jax
import jax.numpy as jnp
import numpy as np
from jax import lax

D = 512
K = 64
D_ATOM = 512
BLOCK = 128
EB_DEV = 8
A_DEV = 32
SEG_MOST = 8
EDGES = 16384
ROWS_DEV = 512
P_DEV = 24
PARTS_SIZE = 384
CAP = 3
GROUPS = 2
SLOTS = 128
ACAP = 16
ATOMS = 1024
N_GRAPH = 16
N_BASIS = 2


def touch_ends(result, stream_key, smallest, high):
    extent = result.shape
    place = [jax.random.randint(jax.random.fold_in(stream_key, axis), (), 0, extent[axis]) for axis in range(len(extent))]
    result = result.at[tuple(place)].set(smallest)
    longest = extent.index(max(extent))
    place[longest] = (place[longest] + 1) % extent[longest]
    return result.at[tuple(place)].set(high)


def block_scale(rng, dims, shards, smallest, high):
    factor_of, own = 1.0, jax.random.fold_in(rng, 6)
    for axis_at, parts in shards:
        heights = jnp.exp(jax.random.uniform(jax.random.fold_in(own, axis_at), (parts,), jnp.float32, smallest / len(shards), high / len(shards)))
        factor_of = factor_of * jnp.repeat(heights, dims[axis_at] // parts).reshape([-1 if axis == axis_at else 1 for axis in range(len(dims))])
    return factor_of


def length_profile(count, total, bound, lean):
    weights = [(1 << 20) // math.isqrt(standing ** lean) + 1 for standing in range(2, count + 1)]
    spare, given = total - bound - (count - 1), [1] * (count - 1)
    while spare > 0:
        movable = [i for i in range(count - 1) if given[i] < bound]
        mass, remaining = sum([weights[i] for i in movable]), spare
        for i in movable:
            more = min(bound - given[i], max(1, remaining * weights[i] // mass), spare)
            given[i] = given[i] + more
            spare = spare - more
    return np.array([bound] + given)


def uneven(rng, amount, total, most, skew):
    if amount == 2:
        one = jax.random.randint(rng, (), max(1, total - most), min(most, total - 1) + 1)
        return jnp.stack([one, total - one])
    sizes = jnp.asarray(length_profile(amount, total, most, skew), jnp.int32)
    couples = (amount - 1) // 2
    donor, receiver = sizes[1:1 + 2 * couples:2], sizes[2:2 + 2 * couples:2]
    room = jnp.minimum(donor - 1, most - receiver)
    passed = jax.random.randint(jax.random.fold_in(rng, 1), (couples,), 0, 1 << 20) % (room + 1)
    sizes = sizes.at[1:1 + 2 * couples:2].set(donor - passed).at[2:2 + 2 * couples:2].set(receiver + passed)
    return sizes[jax.random.permutation(jax.random.fold_in(rng, 2), amount)]


def shared_out(key, own, number, rows, amount, top, reach, lean):
    ranking = jax.random.permutation(key, amount)
    heavy_load, usual = shares(amount, rows * top, reach, lean, True), shares(amount, rows * top, reach, lean, False)
    places = jnp.arange(amount)

    def named(lengths, rotation):
        used = int((lengths > 0).sum())
        fixed = max(1, used // 4)
        shifted = fixed + (places - fixed + rotation * (used - fixed)) % max(1, amount - fixed)
        return jnp.zeros((amount,), jnp.int32).at[ranking[jnp.where(places < fixed, places, shifted)]].set(jnp.asarray(lengths, jnp.int32))

    lengths = jnp.where(number % 4 == 0, named(heavy_load, number // 4), named(usual, number - number // 4 - 1))
    mixed = jax.random.permutation(jax.random.fold_in(own, 3), amount)
    source_of, sink = mixed[0:amount // 2 * 2:2], mixed[1:amount // 2 * 2:2]
    room = jnp.minimum(lengths[source_of] - 1, reach - lengths[sink]) // 2
    room = jnp.where((source_of == ranking[0]) | (sink == ranking[0]) | (lengths[sink] == 0), 0, jnp.maximum(room, 0))
    shifted = jax.random.randint(jax.random.fold_in(own, 4), (amount // 2,), 0, 1 << 20) % (room + 1)
    lengths = lengths.at[source_of].add(-shifted).at[sink].add(shifted)
    members = jnp.searchsorted(jnp.cumsum(lengths), jnp.arange(rows * top), side="right").astype(jnp.int32)
    listing = members.reshape(top, rows).T
    listing = listing[jax.random.permutation(jax.random.fold_in(own, 1), rows)]
    rotation = jax.random.randint(jax.random.fold_in(own, 2), (rows, 1), 0, top)
    return jnp.take_along_axis(listing, (jnp.arange(top)[None, :] + rotation) % top, axis=1)


def shares(count, total, limit, slope, full):
    loads = [(1 << 20) // math.isqrt(rank ** slope) + 1 for rank in range(1, count + 1)]
    largest = limit if full else min(limit, max(-(-total // count), total * loads[0] // sum(loads)))
    least = 1 if total - largest >= count - 1 else 0
    counts, rest = [largest] + [least] * (count - 1), total - largest - least * (count - 1)
    while rest > 0:
        candidates = [i for i in range(1, count) if counts[i] < largest] or [i for i in range(1, count) if counts[i] < limit]
        pool, remaining = sum([loads[i] for i in candidates]), rest
        for i in candidates:
            addition = min(limit - counts[i], max(1, remaining * loads[i] // pool), rest)
            counts[i] = counts[i] + addition
            rest = rest - addition
    return np.array(counts)


def gaussian(own_key, dims, scale, most, split=(), kind=jnp.bfloat16):
    result = jax.random.normal(own_key, dims, jnp.float32) * scale
    if len(split) > 0:
        result = block_scale(own_key, dims, split, -0.22, 0.18) * result
    return jnp.clip(result, min=-most, max=most).astype(kind)


def setup_inputs(seed: int = 0) -> dict:
    arg_keys = jax.random.split(jax.random.key(seed), 17)
    edge_feats = gaussian(arg_keys[0], (EDGES, D), 1.0, 6.0, ((0, 32),))
    pre_weight = gaussian(arg_keys[1], (D, D), D ** -0.5, 0.25)
    down_weight = gaussian(arg_keys[2], (D, K), D ** -0.5, 0.25)
    angle_tiles = gaussian(arg_keys[3], (PARTS_SIZE, GROUPS, BLOCK, BLOCK), BLOCK ** -0.5, 0.5, ((0, 16), (1, 2)))
    part_source = touch_ends(jax.random.randint(arg_keys[4], (PARTS_SIZE,), 0, EB_DEV), jax.random.fold_in(arg_keys[4], 1), 0, EB_DEV - 1).astype(jnp.int32)
    part_owner_keys = jax.random.split(jax.random.fold_in(arg_keys[5], 1), PARTS_SIZE // P_DEV)
    part_owner_turns = jax.random.permutation(jax.random.fold_in(arg_keys[5], 3), PARTS_SIZE // P_DEV)
    part_owner = jax.vmap(lambda own, number: shared_out(jax.random.fold_in(arg_keys[5], 2), own, number, P_DEV, N_GRAPH, 1, CAP, 2))(part_owner_keys, part_owner_turns).reshape((PARTS_SIZE, 1))
    part_target = touch_ends(jax.random.randint(arg_keys[6], (PARTS_SIZE,), 0, EB_DEV), jax.random.fold_in(arg_keys[6], 1), 0, EB_DEV - 1).astype(jnp.int32)
    up_weight = gaussian(arg_keys[7], (GROUPS, K, D), (N_BASIS * K) ** -0.5, 0.5, ((0, 2),))
    res_first = gaussian(arg_keys[8], (D, D), D ** -0.5, 0.25)
    res_second = gaussian(arg_keys[9], (D, D), D ** -0.5, 0.25)
    edge_slot = jax.vmap(lambda own: jnp.searchsorted(jnp.cumsum(uneven(own, SLOTS, ROWS_DEV, SEG_MOST, 1)), jnp.arange(ROWS_DEV), side="right"))(jax.random.split(arg_keys[10], (N_GRAPH * N_BASIS))).reshape((N_GRAPH * N_BASIS, ROWS_DEV)).astype(jnp.int32)
    slot_owner_keys = jax.random.split(jax.random.fold_in(arg_keys[11], 1), (N_GRAPH * N_BASIS) * SLOTS // SLOTS)
    slot_owner_turns = jax.random.permutation(jax.random.fold_in(arg_keys[11], 3), (N_GRAPH * N_BASIS) * SLOTS // SLOTS)
    slot_owner = jax.vmap(lambda own, number: shared_out(jax.random.fold_in(arg_keys[11], 2), own, number, SLOTS, N_GRAPH, 1, ACAP, 1))(slot_owner_keys, slot_owner_turns).reshape((N_GRAPH * N_BASIS, SLOTS, 1))
    slot_atom = touch_ends(jax.random.randint(arg_keys[12], (N_GRAPH * N_BASIS, SLOTS), 0, A_DEV), jax.random.fold_in(arg_keys[12], 1), 0, A_DEV - 1).astype(jnp.int32)
    atom_feats = gaussian(arg_keys[13], (ATOMS, D_ATOM), 1.0, 6.0, ((0, 32),))
    atom_first = gaussian(arg_keys[14], (D, D_ATOM), D ** -0.5, 0.25)
    atom_second = gaussian(arg_keys[15], (D_ATOM, D_ATOM), D_ATOM ** -0.5, 0.25)
    return {"edge_feats": edge_feats, "pre_weight": pre_weight, "down_weight": down_weight, "angle_tiles": angle_tiles, "part_source": part_source, "part_owner": part_owner, "part_target": part_target, "up_weight": up_weight, "res_first": res_first, "res_second": res_second, "edge_slot": edge_slot, "slot_owner": slot_owner, "slot_atom": slot_atom, "atom_feats": atom_feats, "atom_first": atom_first, "atom_second": atom_second}


def reference(edge_feats, pre_weight, down_weight, angle_tiles, part_source, part_owner, part_target, up_weight, res_first, res_second, edge_slot, slot_owner, slot_atom, atom_feats, atom_first, atom_second):
    projected = jax.nn.silu(jnp.dot(edge_feats, pre_weight, preferred_element_type=jnp.float32)).astype(jnp.bfloat16)
    lowered = jax.nn.silu(jnp.dot(projected, down_weight, preferred_element_type=jnp.float32)).astype(jnp.bfloat16)
    blocks = lowered.reshape(N_GRAPH * EB_DEV, BLOCK, K)
    owner_shard = jnp.arange(PARTS_SIZE, dtype=jnp.int32) // P_DEV
    source_block = (owner_shard * EB_DEV + part_source).astype(jnp.int32)
    target_block = (part_owner[:, 0] * EB_DEV + part_target).astype(jnp.int32)
    sources = blocks[source_block].astype(jnp.float32)

    def per_group(group_tiles):
        product = jnp.einsum("pij,pjk->pik", group_tiles.astype(jnp.float32), sources).astype(jnp.bfloat16)
        summed = jax.ops.segment_sum(product.astype(jnp.float32), target_block, num_segments=N_GRAPH * EB_DEV)
        return summed.reshape(EDGES, K).astype(jnp.bfloat16)

    paired = lax.map(per_group, jnp.moveaxis(angle_tiles, 1, 0))
    columns = jnp.moveaxis(paired, 0, 1).reshape(EDGES, GROUPS * K)
    triplet = jnp.dot(columns, up_weight.reshape(GROUPS * K, D), preferred_element_type=jnp.float32)
    joined = (edge_feats.astype(jnp.float32) + triplet).astype(jnp.bfloat16)
    inner = jax.nn.silu(jnp.dot(joined, res_first, preferred_element_type=jnp.float32)).astype(jnp.bfloat16)
    second = jax.nn.silu(jnp.dot(inner, res_second, preferred_element_type=jnp.float32))
    edge_update = ((joined.astype(jnp.float32) + second) * (0.5 ** 0.5)).astype(jnp.bfloat16)
    device_ids = jnp.arange(N_GRAPH * N_BASIS, dtype=jnp.int32)
    slot_ids = (device_ids[:, None] * SLOTS + edge_slot).reshape(-1).astype(jnp.int32)
    slot_sums = jax.ops.segment_sum(edge_update.astype(jnp.float32), slot_ids, num_segments=N_GRAPH * N_BASIS * SLOTS).astype(jnp.bfloat16)
    atom_ids = (slot_owner[:, :, 0] * N_BASIS + (device_ids % N_BASIS)[:, None]) * A_DEV + slot_atom
    gathered = jax.ops.segment_sum(slot_sums.astype(jnp.float32), atom_ids.reshape(-1).astype(jnp.int32), num_segments=ATOMS).astype(jnp.bfloat16)
    hidden = jax.nn.silu(jnp.dot(gathered, atom_first, preferred_element_type=jnp.float32)).astype(jnp.bfloat16)
    atom_update = (atom_feats.astype(jnp.float32) + jnp.dot(hidden, atom_second, preferred_element_type=jnp.float32)).astype(jnp.bfloat16)
    return edge_update, atom_update
```

```python
import functools

import jax
import jax.numpy as jnp
from jax import lax
from jax.experimental import pallas as pl
from jax.experimental.pallas import tpu as pltpu
from jax.sharding import PartitionSpec as P

half_root = 0.5**0.5
MESH = pl.DeviceIdType.MESH
bf16 = jnp.bfloat16
f32 = jnp.float32


def dot(a, b):
    return jnp.dot(a, b, preferred_element_type=f32)


def silu(v):
    return v / (1.0 + jnp.exp(-v))


def kernel(
    n, groups, cap, acap, parts, nb, block, tile_rows,
    scal, meta, owner_col, edge_slot,
    feats_h, pre_h, down_h, angle_h, up_h, first_h, second_h, afeats_h, afirst_h, asecond_h,
    edge_out, atom_out,
    feats, pre, down, angle, up_all, first, second, afeats, afirst, asecond,
    low_all, diag, prod, part_send, part_recv, meta_recv, acc, paired, pair_recv,
    atom_send, atom_recv,
    load_sem, meta_ss, meta_rs, part_ss, part_rs, atom_ss, atom_rs,
    low_ss, low_rs, up_ss, up_rs, pair_ss, pair_rs,
):
    me = lax.axis_index("graph")
    mine = lax.axis_index("basis")
    half = block // 2
    width = 2 * low_all.shape[3] // 2

    loads = [
        pltpu.make_async_copy(src, dst, load_sem.at[i])
        for i, (src, dst) in enumerate(
            [
                (feats_h, feats), (pre_h, pre), (down_h, down), (angle_h, angle),
                (up_h.at[0], up_all.at[mine]), (first_h, first), (second_h, second),
                (afeats_h, afeats), (afirst_h, afirst), (asecond_h, asecond),
            ]
        )
    ]
    for load in loads:
        load.start()

    barrier = pltpu.get_barrier_semaphore()

    def greet(k, carry):
        pl.semaphore_signal(
            barrier, inc=1, device_id=(lax.rem(me + k, n), mine), device_id_type=MESH
        )
        return carry

    lax.fori_loop(1, n, greet, 0)
    for k in range(1, groups):
        pl.semaphore_signal(
            barrier, inc=1, device_id=(me, lax.rem(mine + k, groups)), device_id_type=MESH
        )

    def send(src, dst, ss, rs, to, to_basis):
        return pltpu.make_async_remote_copy(
            src_ref=src, dst_ref=dst, send_sem=ss, recv_sem=rs,
            device_id=(to, to_basis), device_id_type=MESH,
        )

    def meta_copy(d, slot):
        return send(meta.at[d], meta_recv.at[slot], meta_ss.at[d], meta_rs.at[slot], d, mine)

    def part_copy(d, slot):
        return send(
            part_send.at[d], part_recv.at[slot], part_ss.at[d], part_rs.at[slot], d, mine
        )

    def atom_copy(d, slot):
        return send(
            atom_send.at[d], atom_recv.at[slot], atom_ss.at[d], atom_rs.at[slot], d, mine
        )

    def up_copy(g, slot):
        return send(up_h.at[0], up_all.at[slot], up_ss.at[g], up_rs.at[slot], me, g)

    def low_copy(g, slot):
        return send(low_all.at[mine], low_all.at[slot], low_ss.at[g], low_rs.at[slot], me, g)

    def pair_copy(g, slot):
        return send(paired.at[g], pair_recv.at[slot], pair_ss.at[g], pair_rs.at[slot], me, g)

    loads[0].wait()
    loads[1].wait()
    projected = silu(dot(feats[...], pre[...])).astype(bf16)
    loads[2].wait()
    down_twice = jnp.concatenate([down[...], down[...]], axis=1)
    lowered = silu(dot(projected, down_twice)).reshape(nb, 2, half, width)
    lane = lax.broadcasted_iota(jnp.int32, (nb, half, width), 2)
    low_all[mine] = jnp.where(lane < width // 2, lowered[:, 0], lowered[:, 1]).astype(bf16)

    pl.semaphore_wait(barrier, n - 1 + groups - 1)
    others = [lax.rem(mine + k, groups) for k in range(1, groups)]
    for g in others:
        low_copy(g, mine).start()

    def start_meta(k, carry):
        meta_copy(lax.rem(me + k, n), me).start()
        return carry

    lax.fori_loop(1, n, start_meta, 0)
    for g in others:
        up_copy(g, mine).start()
    meta_recv[me] = meta[me]

    def spread(g):
        lane = lax.broadcasted_iota(jnp.int32, (half, width), 1)
        left = lane < width // 2
        for i in range(nb):
            packed = low_all[g, i].astype(f32)
            turned = pltpu.roll(packed, width // 2, 1)
            at = g * nb + i
            diag[at, 0:half] = jnp.where(left, packed, 0.0).astype(bf16)
            diag[at, half : 2 * half] = jnp.where(left, turned, 0.0).astype(bf16)
            diag[at, 2 * half : 3 * half] = jnp.where(left, 0.0, turned).astype(bf16)
            diag[at, 3 * half :] = jnp.where(left, 0.0, packed).astype(bf16)

    spread(mine)
    loads[3].wait()
    for g in others:
        low_copy(g, g).wait_recv()
        spread(g)

    for p in range(parts):
        tile = angle[p, 0]
        wide = jnp.concatenate([tile[:half], tile[half:]], axis=1)
        prod[p] = dot(wide, diag[scal[p]]).astype(bf16)

    def fill(d, ref, slot):
        for s in range(cap):
            ref[slot, s] = prod[scal[parts + d * cap + s]]

    def start_part(i, carry):
        for k in (n // 2 + i, n // 2 - i):
            d = lax.rem(me + k, n)
            fill(d, part_send, d)
            part_copy(d, me).start()
        return carry

    d = lax.rem(me + n // 2, n)
    fill(d, part_send, d)
    part_copy(d, me).start()
    lax.fori_loop(1, n // 2, start_part, 0)
    fill(me, part_recv, me)

    acc[...] = jnp.zeros_like(acc)

    def add(src):
        targets = [meta_recv[src, s : s + 1, :] for s in range(cap)]
        arrived = [part_recv[src, s].astype(f32) for s in range(cap)]
        for j in range(groups * nb):
            total = acc[j]
            for t, a in zip(targets, arrived):
                total = total + jnp.where(jnp.broadcast_to(t == j, a.shape), a, 0.0)
            acc[j] = total

    add(me)

    def take(i, carry):
        src = lax.rem(me + i, n)
        meta_copy(src, src).wait_recv()
        part_copy(src, src).wait_recv()
        add(src)
        return carry

    lax.fori_loop(1, n, take, 0)

    rows_half = nb * half
    for g in range(groups):
        paired[g] = acc[g * nb : (g + 1) * nb].reshape(rows_half, width).astype(bf16)
    for g in others:
        pair_copy(g, mine).start()
    pair_recv[mine] = paired[mine]

    loads[4].wait()
    for g in others:
        up_copy(g, g).wait_recv()
    blank = jnp.zeros(up_all.shape[1:], bf16)
    above = jnp.concatenate([x for g in range(groups) for x in (up_all[g], blank)], axis=0)
    below = jnp.concatenate([x for g in range(groups) for x in (blank, up_all[g])], axis=0)
    pick = (owner_col[...] == edge_slot[...]).astype(f32).astype(bf16)
    loads[5].wait()
    loads[6].wait()
    for g in others:
        pair_copy(g, g).wait_recv()
    columns = jnp.concatenate([pair_recv[g] for g in range(groups)], axis=1)
    upper = dot(columns, above).reshape(nb, 1, half, above.shape[1])
    lower = dot(columns, below).reshape(nb, 1, half, above.shape[1])
    triplet = jnp.concatenate([upper, lower], axis=1).reshape(feats.shape)
    joined = (feats[...].astype(f32) + triplet).astype(bf16)
    inner = silu(dot(joined, first[...])).astype(bf16)
    deep = silu(dot(inner, second[...]))
    update = ((joined.astype(f32) + deep) * half_root).astype(bf16)
    edge_out[...] = update

    atom_send[...] = dot(pick, update).astype(bf16).reshape(atom_send.shape)

    def start_atom(i, carry):
        for k in (n // 2 + i, n // 2 - i):
            atom_copy(lax.rem(me + k, n), me).start()
        return carry

    atom_copy(lax.rem(me + n // 2, n), me).start()
    lax.fori_loop(1, n // 2, start_atom, 0)
    atom_recv[me] = atom_send[me]

    named = jnp.sum(meta_recv[...], axis=0)[tile_rows:]
    atoms = afeats.shape[0]
    chunks = n * acap // 128
    ids = lax.broadcasted_iota(jnp.int32, (atoms, 128), 0) + 1
    chosen = jnp.concatenate(
        [(ids == named[r : r + 1]).astype(f32).astype(bf16) for r in range(chunks)], axis=1
    )
    for load in loads[7:]:
        load.wait()

    def take_atom(i, carry):
        src = lax.rem(me + i, n)
        atom_copy(src, src).wait_recv()
        return carry

    lax.fori_loop(1, n, take_atom, 0)
    gathered = dot(chosen, atom_recv[...].reshape(n * acap, atom_recv.shape[2])).astype(bf16)
    hidden = silu(dot(gathered, afirst[...])).astype(bf16)
    atom_out[...] = (afeats[...].astype(f32) + dot(hidden, asecond[...])).astype(bf16)

    def finish(k, carry):
        d = lax.rem(me + k, n)
        meta_copy(d, me).wait_send()
        part_copy(d, me).wait_send()
        atom_copy(d, me).wait_send()
        return carry

    lax.fori_loop(1, n, finish, 0)
    for g in others:
        low_copy(g, mine).wait_send()
        up_copy(g, mine).wait_send()
        pair_copy(g, mine).wait_send()


def slot_table(target, peers, capacity, stride, values):
    count = target.shape[0]
    ids = jnp.arange(count, dtype=jnp.int32)
    same = (target[:, None] == target[None, :]) & (ids[None, :] < ids[:, None])
    rank = jnp.sum(same.astype(jnp.int32), axis=1)
    place = target * stride + rank
    slots = jnp.arange(peers * stride, dtype=jnp.int32)
    match = place[None, :] == slots[:, None]
    items = jnp.sum(jnp.where(match, ids[None, :] + 1, 0), axis=1) - 1
    picked = jnp.sum(jnp.where(match, values[None, :] + 1, 0), axis=1) - 1
    return items, picked


def body(
    edge_feats, pre_weight, down_weight, angle_tiles, part_source, part_owner, part_target,
    up_weight, res_first, res_second, edge_slot, slot_owner, slot_atom, atom_feats,
    atom_first, atom_second,
):
    n, groups = lax.axis_size("graph"), lax.axis_size("basis")
    me = lax.axis_index("graph")
    parts, _, block, _ = angle_tiles.shape
    narrow = down_weight.shape[1]
    rows, wide = edge_feats.shape
    nb = rows // block
    slot_count = slot_owner.shape[1]
    cap = max(2, 2 * parts // n)
    acap = -(-max(2, 2 * slot_count // n) // 16) * 16

    items, targets = slot_table(part_owner[:, 0], n, cap, cap, part_target)
    scal = jnp.concatenate([part_source, jnp.maximum(items, 0)])
    owners, atoms = slot_table(slot_owner[0, :, 0], n, acap, acap, slot_atom[0])
    tile_rows = cap
    chunk_rows = n * acap // 128
    rows_meta = -(-(cap + chunk_rows) // 8) * 8
    part_rows = jnp.broadcast_to(targets.reshape(n, cap, 1), (n, cap, 128))
    seat = jnp.arange(n, dtype=jnp.int32)[None, :, None] == me
    atom_rows = jnp.where(seat, atoms.reshape(n, 1, acap) + 1, 0).reshape(n, chunk_rows, 128)
    meta = jnp.concatenate(
        [part_rows, atom_rows, jnp.zeros((n, rows_meta - cap - chunk_rows, 128), jnp.int32)],
        axis=1,
    )

    half, pair_width = block // 2, 2 * narrow
    dma = pltpu.SemaphoreType.DMA
    vmem = pl.BlockSpec(memory_space=pltpu.VMEM)
    hbm = pl.BlockSpec(memory_space=pl.ANY)
    scratch = [
        pltpu.VMEM(edge_feats.shape, bf16),
        pltpu.VMEM(pre_weight.shape, bf16),
        pltpu.VMEM(down_weight.shape, bf16),
        pltpu.VMEM(angle_tiles.shape, bf16),
        pltpu.VMEM((groups,) + up_weight.shape[1:], bf16),
        pltpu.VMEM(res_first.shape, bf16),
        pltpu.VMEM(res_second.shape, bf16),
        pltpu.VMEM(atom_feats.shape, bf16),
        pltpu.VMEM(atom_first.shape, bf16),
        pltpu.VMEM(atom_second.shape, bf16),
        pltpu.VMEM((groups, nb, half, pair_width), bf16),
        pltpu.VMEM((groups * nb, 2 * block, pair_width), bf16),
        pltpu.VMEM((parts, half, pair_width), bf16),
        pltpu.VMEM((n, cap, half, pair_width), bf16),
        pltpu.VMEM((n, cap, half, pair_width), bf16),
        pltpu.VMEM((n, rows_meta, 128), jnp.int32),
        pltpu.VMEM((groups * nb, half, pair_width), f32),
        pltpu.VMEM((groups, nb * half, pair_width), bf16),
        pltpu.VMEM((groups, nb * half, pair_width), bf16),
        pltpu.VMEM((n, acap, wide), bf16),
        pltpu.VMEM((n, acap, wide), bf16),
        dma((10,)),
    ] + [dma((n,))] * 6 + [dma((groups,))] * 6
    return pl.pallas_call(
        functools.partial(kernel, n, groups, cap, acap, parts, nb, block, tile_rows),
        out_shape=(
            jax.ShapeDtypeStruct(edge_feats.shape, bf16),
            jax.ShapeDtypeStruct(atom_feats.shape, bf16),
        ),
        in_specs=[pl.BlockSpec(memory_space=pltpu.SMEM), vmem, vmem, vmem] + [hbm] * 10,
        out_specs=(vmem, vmem),
        scratch_shapes=scratch,
        compiler_params=pltpu.CompilerParams(
            collective_id=0, has_side_effects=True, vmem_limit_bytes=40 * 2**20
        ),
    )(
        scal, meta, owners[:, None], edge_slot, edge_feats, pre_weight, down_weight,
        angle_tiles, up_weight, res_first, res_second, atom_feats, atom_first, atom_second,
    )


def solution(mesh):
    rows = P(("graph", "basis"), None)
    in_specs = (
        rows,
        P(),
        P(),
        P("graph", "basis", None, None),
        P("graph"),
        P("graph", None),
        P("graph"),
        P("basis", None, None),
        P(),
        P(),
        rows,
        P(("graph", "basis"), None, None),
        rows,
        rows,
        P(),
        P(),
    )
    return jax.shard_map(
        body, mesh=mesh, in_specs=in_specs, out_specs=(rows, rows), check_vma=False
    )
```

```python
import functools

import jax
import jax.numpy as jnp
from jax import lax
from jax.experimental import pallas as pl
from jax.experimental.pallas import tpu as pltpu
from jax.sharding import PartitionSpec as P

half_root = 0.5**0.5
MESH = pl.DeviceIdType.MESH
bf16 = jnp.bfloat16
f32 = jnp.float32


def dot(a, b):
    return jnp.dot(a, b, preferred_element_type=f32)


def silu(v):
    return v / (1.0 + jnp.exp(-v))


def lines(shape, axis):
    return lax.broadcasted_iota(jnp.int32, shape, axis)


def ranks(row):
    count = row.shape[1]
    down, along = lines((count, count), 0), lines((count, count), 1)
    col = jnp.sum(jnp.where(down == along, row, 0), axis=1, keepdims=True)
    same = jnp.where(col == row, 1, 0)
    rank_row = jnp.sum(jnp.where(down < along, same, 0), axis=0, keepdims=True)
    rank_col = jnp.sum(jnp.where(along < down, same, 0), axis=1, keepdims=True)
    return col, rank_row, rank_col


def kernel(
    n, groups, cap, acap, seat, chunks, nb, block,
    part_source, part_owner, part_target, slot_owner, slot_atom, edge_slot,
    feats_h, pre_h, down_h, angle_h, up_h, first_h, second_h, afeats_h, afirst_h, asecond_h,
    edge_out, atom_out,
    feats, pre, down, angle, up_all, first, second, afeats, afirst, asecond,
    low_all, diag, prod, part_send, part_recv, meta, meta_recv, items_v, items, acc, paired,
    pair_recv, pick, atom_send, atom_recv,
    load_sem, item_sem, meta_ss, meta_rs, part_ss, part_rs, atom_ss, atom_rs,
    low_ss, low_rs, up_ss, up_rs, pair_ss, pair_rs,
):
    me = lax.axis_index("graph")
    mine = lax.axis_index("basis")
    half = block // 2
    width = 2 * low_all.shape[3] // 2

    loads = [
        pltpu.make_async_copy(src, dst, load_sem.at[i])
        for i, (src, dst) in enumerate(
            [
                (feats_h, feats), (pre_h, pre), (down_h, down), (angle_h, angle),
                (up_h.at[0], up_all.at[mine]), (first_h, first), (second_h, second),
                (afeats_h, afeats), (afirst_h, afirst), (asecond_h, asecond),
            ]
        )
    ]
    for load in loads:
        load.start()

    barrier = pltpu.get_barrier_semaphore()

    def greet(k, carry):
        pl.semaphore_signal(
            barrier, inc=1, device_id=(lax.rem(me + k, n), mine), device_id_type=MESH
        )
        return carry

    lax.fori_loop(1, n, greet, 0)
    for k in range(1, groups):
        pl.semaphore_signal(
            barrier, inc=1, device_id=(me, lax.rem(mine + k, groups)), device_id_type=MESH
        )

    def send(src, dst, ss, rs, to, to_basis):
        return pltpu.make_async_remote_copy(
            src_ref=src, dst_ref=dst, send_sem=ss, recv_sem=rs,
            device_id=(to, to_basis), device_id_type=MESH,
        )

    def meta_copy(d, slot):
        return send(meta.at[d], meta_recv.at[slot], meta_ss.at[d], meta_rs.at[slot], d, mine)

    def part_copy(h, d, slot):
        return send(
            part_send.at[h, d], part_recv.at[h, slot], part_ss.at[h, d], part_rs.at[h, slot],
            d, mine,
        )

    def atom_copy(d, slot):
        return send(
            atom_send.at[d], atom_recv.at[slot], atom_ss.at[d], atom_rs.at[slot], d, mine
        )

    def up_copy(g, slot):
        return send(up_h.at[0], up_all.at[slot], up_ss.at[g], up_rs.at[slot], me, g)

    def low_copy(g, slot):
        return send(low_all.at[mine], low_all.at[slot], low_ss.at[g], low_rs.at[slot], me, g)

    def pair_copy(h, g, slot):
        return send(
            paired.at[h, g], pair_recv.at[h, slot], pair_ss.at[h, g], pair_rs.at[h, slot], me, g
        )

    parts = part_owner.shape[1]
    owner = part_owner[...]
    owner_col, rank_row, rank_col = ranks(owner)
    match = lines((n * seat, parts), 0) == owner * seat + rank_row
    goal = jnp.sum(
        jnp.where(match, part_target[...] + 1, 0), axis=1, keepdims=True
    )
    spread_goal = jnp.broadcast_to(goal - 1, (n * seat, 128))
    meta[:, 0:seat, :] = spread_goal.reshape(n, seat, 128)
    match = lines((parts, n * seat), 1) == owner_col * seat + rank_col
    items_v[...] = jnp.sum(
        jnp.where(match, lines((parts, n * seat), 0), 0), axis=0, keepdims=True
    )
    item_copy = pltpu.make_async_copy(items_v, items, item_sem.at[0])
    item_copy.start()

    slots = slot_owner.shape[1]
    owner = slot_owner[...]
    owner_col, rank_row, rank_col = ranks(owner)
    match = lines((n * acap, slots), 0) == owner * acap + rank_row
    held = jnp.sum(
        jnp.where(match, lines((n * acap, slots), 1) + 1, 0), axis=1, keepdims=True
    )
    pick[...] = (held - 1 == edge_slot[...]).astype(f32).astype(bf16)
    wanted = jnp.where(
        lines((n, slots), 0) == owner, slot_atom[...].astype(f32) + 1.0, 0.0
    ).astype(bf16)
    first_lane = me * acap
    lanes = (lines((slots, n * acap), 1) == rank_col + first_lane).astype(f32).astype(bf16)
    atom_meta = dot(wanted, lanes).astype(jnp.int32)
    for r in range(chunks):
        meta[:, seat + r, :] = atom_meta[:, r * 128 : (r + 1) * 128]

    loads[0].wait()
    loads[1].wait()
    projected = silu(dot(feats[...], pre[...])).astype(bf16)
    loads[2].wait()
    down_twice = jnp.concatenate([down[...], down[...]], axis=0)
    lowered = silu(
        lax.dot_general(
            projected, down_twice, (((1,), (1,)), ((), ())), preferred_element_type=f32
        )
    ).reshape(nb, 2, half, width)
    lane = lax.broadcasted_iota(jnp.int32, (nb, half, width), 2)
    low_all[mine] = jnp.where(lane < width // 2, lowered[:, 0], lowered[:, 1]).astype(bf16)

    pl.semaphore_wait(barrier, n - 1 + groups - 1)
    others = [lax.rem(mine + k, groups) for k in range(1, groups)]
    for g in others:
        low_copy(g, mine).start()

    def start_meta(k, carry):
        meta_copy(lax.rem(me + k, n), me).start()
        return carry

    lax.fori_loop(1, n, start_meta, 0)
    for g in others:
        up_copy(g, mine).start()
    meta_recv[me] = meta[me]

    def spread(g):
        lane = lax.broadcasted_iota(jnp.int32, (half, width), 1)
        left = lane < width // 2
        for i in range(nb):
            packed = low_all[g, i].astype(f32)
            turned = pltpu.roll(packed, width // 2, 1)
            at = g * nb + i
            diag[at, 0:half] = jnp.where(left, packed, 0.0).astype(bf16)
            diag[at, half : 2 * half] = jnp.where(left, turned, 0.0).astype(bf16)
            diag[at, 2 * half : 3 * half] = jnp.where(left, 0.0, turned).astype(bf16)
            diag[at, 3 * half :] = jnp.where(left, 0.0, packed).astype(bf16)

    spread(mine)
    loads[3].wait()
    for g in others:
        low_copy(g, g).wait_recv()
        spread(g)

    for p in range(parts):
        tile = angle[p, 0]
        wide = jnp.concatenate([tile[:half], tile[half:]], axis=1)
        prod[p] = dot(wide, diag[part_source[p]]).astype(bf16)
    item_copy.wait()

    pieces = part_send.shape[0]
    piece = half // pieces

    def fill(h, d, ref, slot):
        for s in range(cap):
            ref[h, slot, s] = prod[jnp.clip(items[0, d * seat + s], 0, prod.shape[0] - 1), h * piece : (h + 1) * piece]

    def start_part(h, k):
        d = lax.rem(me + k, n)
        fill(h, d, part_send, d)
        part_copy(h, d, me).start()

    for h in range(pieces):

        def start_two(i, carry):
            start_part(h, n // 2 + i)
            start_part(h, n // 2 - i)
            return carry

        start_part(h, n // 2)
        lax.fori_loop(1, n // 2, start_two, 0)
    for h in range(pieces):
        fill(h, me, part_recv, me)

    loads[4].wait()
    for g in others:
        up_copy(g, g).wait_recv()
    blank = jnp.zeros(up_all.shape[1:], bf16)
    above = jnp.concatenate([x for g in range(groups) for x in (up_all[g], blank)], axis=0)
    below = jnp.concatenate([x for g in range(groups) for x in (blank, up_all[g])], axis=0)
    for load in loads[5:]:
        load.wait()

    acc[...] = jnp.zeros_like(acc)

    def add(h, src):
        targets = [meta_recv[src, s : s + 1, :] for s in range(cap)]
        arrived = [part_recv[h, src, s].astype(f32) for s in range(cap)]
        for j in range(groups * nb):
            total = acc[h, j]
            for t, a in zip(targets, arrived):
                total = total + jnp.where(jnp.broadcast_to(t == j, a.shape), a, 0.0)
            acc[h, j] = total

    depth = above.shape[1]
    for h in range(pieces):
        add(h, me)

        def take(i, carry):
            src = lax.rem(me + i, n)
            if h == 0:
                meta_copy(src, src).wait_recv()
            part_copy(h, src, src).wait_recv()
            add(h, src)
            return carry

        lax.fori_loop(1, n, take, 0)
        for g in range(groups):
            paired[h, g] = acc[h, g * nb : (g + 1) * nb].reshape(nb * piece, width).astype(bf16)
        for g in others:
            pair_copy(h, g, mine).start()
        pair_recv[h, mine] = paired[h, mine]
        for g in others:
            pair_copy(h, g, g).wait_recv()

        columns = jnp.concatenate([pair_recv[h, g] for g in range(groups)], axis=1)
        upper = dot(columns, above).reshape(nb, 1, piece, depth)
        lower = dot(columns, below).reshape(nb, 1, piece, depth)
        triplet = jnp.concatenate([upper, lower], axis=1).reshape(2 * nb * piece, depth)
        starts = [q * half + h * piece for q in range(2 * nb)]
        own = jnp.concatenate([feats[at : at + piece] for at in starts], axis=0)
        joined = (own.astype(f32) + triplet).astype(bf16)
        inner = silu(dot(joined, first[...])).astype(bf16)
        deep = silu(dot(inner, second[...]))
        update = ((joined.astype(f32) + deep) * half_root).astype(bf16)
        for q, at in enumerate(starts):
            edge_out[at : at + piece] = update[q * piece : (q + 1) * piece]

    atom_send[...] = dot(pick[...], edge_out[...]).astype(bf16).reshape(atom_send.shape)

    def start_atom(i, carry):
        for k in (n // 2 + i, n // 2 - i):
            atom_copy(lax.rem(me + k, n), me).start()
        return carry

    atom_copy(lax.rem(me + n // 2, n), me).start()
    lax.fori_loop(1, n // 2, start_atom, 0)
    atom_recv[me] = atom_send[me]

    named = jnp.sum(meta_recv[...], axis=0)[seat:]
    atoms = afeats.shape[0]
    ids = lax.broadcasted_iota(jnp.int32, (atoms, 128), 0) + 1
    chosen = jnp.concatenate(
        [(ids == named[r : r + 1]).astype(f32).astype(bf16) for r in range(chunks)], axis=1
    )
    def take_atom(i, carry):
        src = lax.rem(me + i, n)
        atom_copy(src, src).wait_recv()
        return carry

    lax.fori_loop(1, n, take_atom, 0)
    gathered = dot(chosen, atom_recv[...].reshape(n * acap, atom_recv.shape[2])).astype(bf16)
    hidden = silu(dot(gathered, afirst[...])).astype(bf16)
    atom_out[...] = (afeats[...].astype(f32) + dot(hidden, asecond[...])).astype(bf16)

    def finish(k, carry):
        d = lax.rem(me + k, n)
        meta_copy(d, me).wait_send()
        for h in range(pieces):
            part_copy(h, d, me).wait_send()
        atom_copy(d, me).wait_send()
        return carry

    lax.fori_loop(1, n, finish, 0)
    for g in others:
        low_copy(g, mine).wait_send()
        up_copy(g, mine).wait_send()
        for h in range(pieces):
            pair_copy(h, g, mine).wait_send()


def body(
    edge_feats, pre_weight, down_weight, angle_tiles, part_source, part_owner, part_target,
    up_weight, res_first, res_second, edge_slot, slot_owner, slot_atom, atom_feats,
    atom_first, atom_second,
):
    n, groups = lax.axis_size("graph"), lax.axis_size("basis")
    parts, _, block, _ = angle_tiles.shape
    narrow = down_weight.shape[1]
    rows, wide = edge_feats.shape
    nb = rows // block
    slot_count = slot_owner.shape[1]
    cap = max(2, 2 * parts // n)
    acap = -(-max(2, 2 * slot_count // n) // 16) * 16

    seat = -(-cap // 8) * 8
    chunks = n * acap // 128
    meta_rows = seat + -(-chunks // 8) * 8
    pieces = 2

    half, pair_width = block // 2, 2 * narrow
    dma = pltpu.SemaphoreType.DMA
    vmem = pl.BlockSpec(memory_space=pltpu.VMEM)
    hbm = pl.BlockSpec(memory_space=pl.ANY)
    scratch = [
        pltpu.VMEM(edge_feats.shape, bf16),
        pltpu.VMEM(pre_weight.shape, bf16),
        pltpu.VMEM(down_weight.shape[::-1], bf16),
        pltpu.VMEM(angle_tiles.shape, bf16),
        pltpu.VMEM((groups,) + up_weight.shape[1:], bf16),
        pltpu.VMEM(res_first.shape, bf16),
        pltpu.VMEM(res_second.shape, bf16),
        pltpu.VMEM(atom_feats.shape, bf16),
        pltpu.VMEM(atom_first.shape, bf16),
        pltpu.VMEM(atom_second.shape, bf16),
        pltpu.VMEM((groups, nb, half, pair_width), bf16),
        pltpu.VMEM((groups * nb, 2 * block, pair_width), bf16),
        pltpu.VMEM((parts, half, pair_width), bf16),
        pltpu.VMEM((pieces, n, cap, half // pieces, pair_width), bf16),
        pltpu.VMEM((pieces, n, cap, half // pieces, pair_width), bf16),
        pltpu.VMEM((n, meta_rows, 128), jnp.int32),
        pltpu.VMEM((n, meta_rows, 128), jnp.int32),
        pltpu.VMEM((1, n * seat), jnp.int32),
        pltpu.SMEM((1, n * seat), jnp.int32),
        pltpu.VMEM((pieces, groups * nb, half // pieces, pair_width), f32),
        pltpu.VMEM((pieces, groups, nb * half // pieces, pair_width), bf16),
        pltpu.VMEM((pieces, groups, nb * half // pieces, pair_width), bf16),
        pltpu.VMEM((n * acap, rows), bf16),
        pltpu.VMEM((n, acap, wide), bf16),
        pltpu.VMEM((n, acap, wide), bf16),
        dma((10,)),
        dma((1,)),
    ]
    scratch += [dma((n,))] * 2 + [dma((pieces, n))] * 2 + [dma((n,))] * 2
    scratch += [dma((groups,))] * 4 + [dma((pieces, groups))] * 2
    return pl.pallas_call(
        functools.partial(kernel, n, groups, cap, acap, seat, chunks, nb, block),
        out_shape=(
            jax.ShapeDtypeStruct(edge_feats.shape, bf16),
            jax.ShapeDtypeStruct(atom_feats.shape, bf16),
        ),
        in_specs=[pl.BlockSpec(memory_space=pltpu.SMEM)] + [vmem] * 5 + [hbm] * 10,
        out_specs=(vmem, vmem),
        scratch_shapes=scratch,
        compiler_params=pltpu.CompilerParams(
            collective_id=0, has_side_effects=True, vmem_limit_bytes=62 * 2**20
        ),
    )(
        part_source, part_owner.reshape(1, parts), part_target.reshape(1, parts),
        slot_owner.reshape(1, slot_count), slot_atom, edge_slot,
        edge_feats, pre_weight, down_weight.T,
        angle_tiles, up_weight, res_first, res_second, atom_feats, atom_first, atom_second,
    )


def solution(mesh):
    rows = P(("graph", "basis"), None)
    in_specs = (
        rows,
        P(),
        P(),
        P("graph", "basis", None, None),
        P("graph"),
        P("graph", None),
        P("graph"),
        P("basis", None, None),
        P(),
        P(),
        rows,
        P(("graph", "basis"), None, None),
        rows,
        rows,
        P(),
        P(),
    )
    return jax.shard_map(
        body, mesh=mesh, in_specs=in_specs, out_specs=(rows, rows), check_vma=False
    )
```

```python
import functools

import jax
import jax.numpy as jnp
from jax import lax
from jax.experimental import pallas as pl
from jax.experimental.pallas import tpu as pltpu
from jax.sharding import PartitionSpec as P

half_root = 0.5**0.5
MESH = pl.DeviceIdType.MESH
bf16 = jnp.bfloat16
f32 = jnp.float32


def dot(a, b):
    return jnp.dot(a, b, preferred_element_type=f32)


def silu(v):
    return v / (1.0 + jnp.exp(-v))


def lines(shape, axis):
    return lax.broadcasted_iota(jnp.int32, shape, axis)


def ranks(row):
    count = row.shape[1]
    down, along = lines((count, count), 0), lines((count, count), 1)
    col = jnp.sum(jnp.where(down == along, row, 0), axis=1, keepdims=True)
    same = jnp.where(col == row, 1, 0)
    rank_row = jnp.sum(jnp.where(down < along, same, 0), axis=0, keepdims=True)
    rank_col = jnp.sum(jnp.where(along < down, same, 0), axis=1, keepdims=True)
    return col, rank_row, rank_col


def kernel(
    n, groups, cap, acap, seat, chunks, nb, block,
    part_source, part_owner, part_target, slot_owner, slot_atom, edge_slot,
    feats_h, pre_h, down_h, angle_h, up_h, first_h, second_h, afeats_h, afirst_h, asecond_h,
    edge_h, atom_out,
    edge_out,
    feats, pre, down, angle, up_all, first, second, afeats, afirst, asecond,
    low_all, diag, prod, part_send, part_recv, meta, meta_recv, items_v, items, acc, paired,
    pair_recv, pick, atom_send, atom_recv,
    load_sem, item_sem, edge_sem, meta_ss, meta_rs, part_ss, part_rs, atom_ss, atom_rs,
    low_ss, low_rs, up_ss, up_rs, pair_ss, pair_rs,
):
    me = lax.axis_index("graph")
    mine = lax.axis_index("basis")
    half = block // 2
    width = 2 * low_all.shape[3] // 2

    loads = [
        pltpu.make_async_copy(src, dst, load_sem.at[i])
        for i, (src, dst) in enumerate(
            [
                (feats_h, feats), (pre_h, pre), (down_h, down), (angle_h, angle),
                (up_h.at[0], up_all.at[mine]), (first_h, first), (second_h, second),
                (afeats_h, afeats), (afirst_h, afirst), (asecond_h, asecond),
            ]
        )
    ]
    for load in loads[:3]:
        load.start()

    barrier = pltpu.get_barrier_semaphore()

    def greet(k, carry):
        pl.semaphore_signal(
            barrier, inc=1, device_id=(lax.rem(me + k, n), mine), device_id_type=MESH
        )
        return carry

    lax.fori_loop(1, n, greet, 0)
    for k in range(1, groups):
        pl.semaphore_signal(
            barrier, inc=1, device_id=(me, lax.rem(mine + k, groups)), device_id_type=MESH
        )

    def send(src, dst, ss, rs, to, to_basis):
        return pltpu.make_async_remote_copy(
            src_ref=src, dst_ref=dst, send_sem=ss, recv_sem=rs,
            device_id=(to, to_basis), device_id_type=MESH,
        )

    def meta_copy(d, slot):
        return send(meta.at[d], meta_recv.at[slot], meta_ss.at[d], meta_rs.at[slot], d, mine)

    def part_copy(h, d, slot):
        return send(
            part_send.at[h, d], part_recv.at[h, slot], part_ss.at[h, d], part_rs.at[h, slot],
            d, mine,
        )

    def atom_copy(d, slot):
        return send(
            atom_send.at[d], atom_recv.at[slot], atom_ss.at[d], atom_rs.at[slot], d, mine
        )

    def up_copy(g, slot):
        return send(up_h.at[0], up_all.at[slot], up_ss.at[g], up_rs.at[slot], me, g)

    def low_copy(g, slot):
        return send(low_all.at[mine], low_all.at[slot], low_ss.at[g], low_rs.at[slot], me, g)

    def pair_copy(h, g, slot):
        return send(
            paired.at[h, g], pair_recv.at[h, slot], pair_ss.at[h, g], pair_rs.at[h, slot], me, g
        )

    loads[0].wait()
    loads[1].wait()
    for load in loads[3:]:
        load.start()
    projected = silu(dot(feats[...], pre[...])).astype(bf16)
    loads[2].wait()
    down_twice = jnp.concatenate([down[...], down[...]], axis=0)
    lowered = silu(
        lax.dot_general(
            projected, down_twice, (((1,), (1,)), ((), ())), preferred_element_type=f32
        )
    ).reshape(nb, 2, half, width)
    lane = lax.broadcasted_iota(jnp.int32, (nb, half, width), 2)
    low_all[mine] = jnp.where(lane < width // 2, lowered[:, 0], lowered[:, 1]).astype(bf16)

    pl.semaphore_wait(barrier, n - 1 + groups - 1)
    others = [lax.rem(mine + k, groups) for k in range(1, groups)]
    for g in others:
        low_copy(g, mine).start()
    for g in others:
        up_copy(g, mine).start()

    parts = part_owner.shape[1]
    owner = part_owner[...]
    owner_col, rank_row, rank_col = ranks(owner)
    match = lines((n * seat, parts), 0) == owner * seat + rank_row
    goal = jnp.sum(
        jnp.where(match, part_target[...] + 1, 0), axis=1, keepdims=True
    )
    spread_goal = jnp.broadcast_to(goal - 1, (n * seat, 128))
    meta[:, 0:seat, :] = spread_goal.reshape(n, seat, 128)
    match = lines((parts, n * seat), 1) == owner_col * seat + rank_col
    items_v[...] = jnp.sum(
        jnp.where(match, lines((parts, n * seat), 0), 0), axis=0, keepdims=True
    )
    item_copy = pltpu.make_async_copy(items_v, items, item_sem.at[0])
    item_copy.start()

    slots = slot_owner.shape[1]
    owner = slot_owner[...]
    owner_col, rank_row, rank_col = ranks(owner)
    match = lines((n * acap, slots), 0) == owner * acap + rank_row
    held = jnp.sum(
        jnp.where(match, lines((n * acap, slots), 1) + 1, 0), axis=1, keepdims=True
    )
    pick[...] = (held - 1 == edge_slot[...]).astype(f32).astype(bf16)
    wanted = jnp.where(
        lines((n, slots), 0) == owner, slot_atom[...].astype(f32) + 1.0, 0.0
    ).astype(bf16)
    first_lane = me * acap
    lanes = (lines((slots, n * acap), 1) == rank_col + first_lane).astype(f32).astype(bf16)
    atom_meta = dot(wanted, lanes).astype(jnp.int32)
    for r in range(chunks):
        meta[:, seat + r, :] = atom_meta[:, r * 128 : (r + 1) * 128]

    def start_meta(k, carry):
        meta_copy(lax.rem(me + k, n), me).start()
        return carry

    lax.fori_loop(1, n, start_meta, 0)
    meta_recv[me] = meta[me]

    def spread(g):
        lane = lax.broadcasted_iota(jnp.int32, (half, width), 1)
        left = lane < width // 2
        for i in range(nb):
            packed = low_all[g, i].astype(f32)
            turned = pltpu.roll(packed, width // 2, 1)
            at = g * nb + i
            diag[at, 0:half] = jnp.where(left, packed, 0.0).astype(bf16)
            diag[at, half : 2 * half] = jnp.where(left, turned, 0.0).astype(bf16)
            diag[at, 2 * half : 3 * half] = jnp.where(left, 0.0, turned).astype(bf16)
            diag[at, 3 * half :] = jnp.where(left, 0.0, packed).astype(bf16)

    spread(mine)
    loads[3].wait()
    for g in others:
        low_copy(g, g).wait_recv()
        spread(g)

    for p in range(parts):
        tile = angle[p, 0]
        wide = jnp.concatenate([tile[:half], tile[half:]], axis=1)
        prod[p] = dot(wide, diag[part_source[p]]).astype(bf16)
    item_copy.wait()

    pieces = part_send.shape[0]
    piece = half // pieces

    def fill(h, d, ref, slot):
        for s in range(cap):
            ref[h, slot, s] = prod[jnp.clip(items[0, d * seat + s], 0, prod.shape[0] - 1), h * piece : (h + 1) * piece]

    def start_part(h, k):
        d = lax.rem(me + k, n)
        fill(h, d, part_send, d)
        part_copy(h, d, me).start()

    for h in range(pieces):

        def start_two(i, carry):
            start_part(h, n // 2 + i)
            start_part(h, n // 2 - i)
            return carry

        start_part(h, n // 2)
        lax.fori_loop(1, n // 2, start_two, 0)
    for h in range(pieces):
        fill(h, me, part_recv, me)

    loads[4].wait()
    for g in others:
        up_copy(g, g).wait_recv()
    blank = jnp.zeros(up_all.shape[1:], bf16)
    above = jnp.concatenate([x for g in range(groups) for x in (up_all[g], blank)], axis=0)
    below = jnp.concatenate([x for g in range(groups) for x in (blank, up_all[g])], axis=0)
    for load in loads[5:]:
        load.wait()

    acc[...] = jnp.zeros_like(acc)

    def add(h, src):
        targets = [meta_recv[src, s : s + 1, :] for s in range(cap)]
        arrived = [part_recv[h, src, s].astype(f32) for s in range(cap)]
        for j in range(groups * nb):
            total = acc[h, j]
            for t, a in zip(targets, arrived):
                total = total + jnp.where(jnp.broadcast_to(t == j, a.shape), a, 0.0)
            acc[h, j] = total

    depth = above.shape[1]
    for h in range(pieces):
        add(h, me)

        def take(i, carry):
            src = lax.rem(me + i, n)
            if h == 0:
                meta_copy(src, src).wait_recv()
            part_copy(h, src, src).wait_recv()
            add(h, src)
            return carry

        lax.fori_loop(1, n, take, 0)
        for g in range(groups):
            paired[h, g] = acc[h, g * nb : (g + 1) * nb].reshape(nb * piece, width).astype(bf16)
        for g in others:
            pair_copy(h, g, mine).start()
        pair_recv[h, mine] = paired[h, mine]
        for g in others:
            pair_copy(h, g, g).wait_recv()

        columns = jnp.concatenate([pair_recv[h, g] for g in range(groups)], axis=1)
        upper = dot(columns, above).reshape(nb, 1, piece, depth)
        lower = dot(columns, below).reshape(nb, 1, piece, depth)
        triplet = jnp.concatenate([upper, lower], axis=1).reshape(2 * nb * piece, depth)
        starts = [q * half + h * piece for q in range(2 * nb)]
        own = jnp.concatenate([feats[at : at + piece] for at in starts], axis=0)
        joined = (own.astype(f32) + triplet).astype(bf16)
        inner = silu(dot(joined, first[...])).astype(bf16)
        deep = silu(dot(inner, second[...]))
        update = ((joined.astype(f32) + deep) * half_root).astype(bf16)
        for q, at in enumerate(starts):
            edge_out[at : at + piece] = update[q * piece : (q + 1) * piece]

    edge_copy = pltpu.make_async_copy(edge_out, edge_h, edge_sem.at[0])
    edge_copy.start()
    atom_send[...] = dot(pick[...], edge_out[...]).astype(bf16).reshape(atom_send.shape)

    def start_atom(i, carry):
        for k in (n // 2 + i, n // 2 - i):
            atom_copy(lax.rem(me + k, n), me).start()
        return carry

    atom_copy(lax.rem(me + n // 2, n), me).start()
    lax.fori_loop(1, n // 2, start_atom, 0)
    atom_recv[me] = atom_send[me]

    named = jnp.sum(meta_recv[...], axis=0)[seat:]
    atoms = afeats.shape[0]
    ids = lax.broadcasted_iota(jnp.int32, (atoms, 128), 0) + 1
    chosen = jnp.concatenate(
        [(ids == named[r : r + 1]).astype(f32).astype(bf16) for r in range(chunks)], axis=1
    )
    def take_atom(i, carry):
        src = lax.rem(me + i, n)
        atom_copy(src, src).wait_recv()
        return carry

    lax.fori_loop(1, n, take_atom, 0)
    gathered = dot(chosen, atom_recv[...].reshape(n * acap, atom_recv.shape[2])).astype(bf16)
    hidden = silu(dot(gathered, afirst[...])).astype(bf16)
    atom_out[...] = (afeats[...].astype(f32) + dot(hidden, asecond[...])).astype(bf16)

    edge_copy.wait()

    def finish(k, carry):
        d = lax.rem(me + k, n)
        meta_copy(d, me).wait_send()
        for h in range(pieces):
            part_copy(h, d, me).wait_send()
        atom_copy(d, me).wait_send()
        return carry

    lax.fori_loop(1, n, finish, 0)
    for g in others:
        low_copy(g, mine).wait_send()
        up_copy(g, mine).wait_send()
        for h in range(pieces):
            pair_copy(h, g, mine).wait_send()


def settle(edge, atom, edge_out, atom_out, sem):
    share = edge.shape[0] // 8
    copies = [
        pltpu.make_async_copy(
            edge.at[i * share : (i + 1) * share], edge_out.at[i * share : (i + 1) * share],
            sem.at[i],
        )
        for i in range(8)
    ] + [pltpu.make_async_copy(atom, atom_out, sem.at[8])]
    for copy in copies:
        copy.start()
    for copy in copies:
        copy.wait()


def body(
    edge_feats, pre_weight, down_weight, angle_tiles, part_source, part_owner, part_target,
    up_weight, res_first, res_second, edge_slot, slot_owner, slot_atom, atom_feats,
    atom_first, atom_second,
):
    n, groups = lax.axis_size("graph"), lax.axis_size("basis")
    parts, _, block, _ = angle_tiles.shape
    narrow = down_weight.shape[1]
    rows, wide = edge_feats.shape
    nb = rows // block
    slot_count = slot_owner.shape[1]
    cap = max(2, 2 * parts // n)
    acap = -(-max(2, 2 * slot_count // n) // 16) * 16

    seat = -(-cap // 8) * 8
    chunks = n * acap // 128
    meta_rows = seat + -(-chunks // 8) * 8
    pieces = 2

    half, pair_width = block // 2, 2 * narrow
    dma = pltpu.SemaphoreType.DMA
    vmem = pl.BlockSpec(memory_space=pltpu.VMEM)
    hbm = pl.BlockSpec(memory_space=pl.ANY)
    scratch = [
        pltpu.VMEM(edge_feats.shape, bf16),
        pltpu.VMEM(edge_feats.shape, bf16),
        pltpu.VMEM(pre_weight.shape, bf16),
        pltpu.VMEM(down_weight.shape[::-1], bf16),
        pltpu.VMEM(angle_tiles.shape, bf16),
        pltpu.VMEM((groups,) + up_weight.shape[1:], bf16),
        pltpu.VMEM(res_first.shape, bf16),
        pltpu.VMEM(res_second.shape, bf16),
        pltpu.VMEM(atom_feats.shape, bf16),
        pltpu.VMEM(atom_first.shape, bf16),
        pltpu.VMEM(atom_second.shape, bf16),
        pltpu.VMEM((groups, nb, half, pair_width), bf16),
        pltpu.VMEM((groups * nb, 2 * block, pair_width), bf16),
        pltpu.VMEM((parts, half, pair_width), bf16),
        pltpu.VMEM((pieces, n, cap, half // pieces, pair_width), bf16),
        pltpu.VMEM((pieces, n, cap, half // pieces, pair_width), bf16),
        pltpu.VMEM((n, meta_rows, 128), jnp.int32),
        pltpu.VMEM((n, meta_rows, 128), jnp.int32),
        pltpu.VMEM((1, n * seat), jnp.int32),
        pltpu.SMEM((1, n * seat), jnp.int32),
        pltpu.VMEM((pieces, groups * nb, half // pieces, pair_width), f32),
        pltpu.VMEM((pieces, groups, nb * half // pieces, pair_width), bf16),
        pltpu.VMEM((pieces, groups, nb * half // pieces, pair_width), bf16),
        pltpu.VMEM((n * acap, rows), bf16),
        pltpu.VMEM((n, acap, wide), bf16),
        pltpu.VMEM((n, acap, wide), bf16),
        dma((10,)),
        dma((1,)),
        dma((1,)),
    ]
    scratch += [dma((n,))] * 2 + [dma((pieces, n))] * 2 + [dma((n,))] * 2
    scratch += [dma((groups,))] * 4 + [dma((pieces, groups))] * 2
    shapes = (
        jax.ShapeDtypeStruct(edge_feats.shape, bf16),
        jax.ShapeDtypeStruct(atom_feats.shape, bf16),
    )
    edge_update, atom_update = pl.pallas_call(
        functools.partial(kernel, n, groups, cap, acap, seat, chunks, nb, block),
        out_shape=shapes,
        in_specs=[pl.BlockSpec(memory_space=pltpu.SMEM)] + [vmem] * 5 + [hbm] * 10,
        out_specs=(hbm, vmem),
        scratch_shapes=scratch,
        compiler_params=pltpu.CompilerParams(
            collective_id=0, has_side_effects=True, vmem_limit_bytes=62 * 2**20
        ),
    )(
        part_source, part_owner.reshape(1, parts), part_target.reshape(1, parts),
        slot_owner.reshape(1, slot_count), slot_atom, edge_slot,
        edge_feats, pre_weight, down_weight.T,
        angle_tiles, up_weight, res_first, res_second, atom_feats, atom_first, atom_second,
    )
    return pl.pallas_call(
        settle,
        out_shape=shapes,
        in_specs=[hbm, hbm],
        out_specs=(hbm, hbm),
        scratch_shapes=[dma((9,))],
        compiler_params=pltpu.CompilerParams(vmem_limit_bytes=62 * 2**20),
    )(edge_update, atom_update)


def solution(mesh):
    rows = P(("graph", "basis"), None)
    in_specs = (
        rows,
        P(),
        P(),
        P("graph", "basis", None, None),
        P("graph"),
        P("graph", None),
        P("graph"),
        P("basis", None, None),
        P(),
        P(),
        rows,
        P(("graph", "basis"), None, None),
        rows,
        rows,
        P(),
        P(),
    )
    return jax.shard_map(
        body, mesh=mesh, in_specs=in_specs, out_specs=(rows, rows), check_vma=False
    )
```

```python
import functools

import jax
import jax.numpy as jnp
from jax import lax
from jax.experimental import pallas as pl
from jax.experimental.pallas import tpu as pltpu
from jax.sharding import PartitionSpec as P

half_root = 0.5**0.5
MESH = pl.DeviceIdType.MESH
bf16 = jnp.bfloat16
f32 = jnp.float32


def dot(a, b):
    return jnp.dot(a, b, preferred_element_type=f32)


def silu(v):
    return v / (1.0 + jnp.exp(-v))


def lines(shape, axis):
    return lax.broadcasted_iota(jnp.int32, shape, axis)


def far_first(count):
    return sorted(range(1, count), key=lambda k: abs(2 * k - count))


def ranks(row):
    count = row.shape[1]
    down, along = lines((count, count), 0), lines((count, count), 1)
    col = jnp.sum(jnp.where(down == along, row, 0), axis=1, keepdims=True)
    same = jnp.where(col == row, 1, 0)
    rank_row = jnp.sum(jnp.where(down < along, same, 0), axis=0, keepdims=True)
    rank_col = jnp.sum(jnp.where(along < down, same, 0), axis=1, keepdims=True)
    return col, rank_row, rank_col


def kernel(
    n, inner, groups, cap, acap, seat, chunks, nb, block,
    part_source, part_owner, part_target, slot_owner, slot_atom, edge_slot,
    feats_h, pre_h, down_h, angle_h, up_h, first_h, second_h,
    edge_h, gathered,
    edge_out,
    feats, pre, down, angle, up_all, first, second,
    low_all, diag, prod, part_send, part_recv, goals, goals_recv, meta, meta_recv, items_v, items,
    plane_send, plane_recv, paired, pair_recv, pick, atom_send, atom_recv,
    load_sem, item_sem, edge_sem, goal_ss, goal_rs, meta_ss, meta_rs, part_ss, part_rs, plane_ss, plane_rs, atom_ss, atom_rs,
    low_ss, low_rs, up_ss, up_rs, pair_ss, pair_rs,
):
    me = lax.axis_index("graph")
    mine = lax.axis_index("basis")
    outer = n // inner
    layer, spot = me // inner, lax.rem(me, inner)
    half = block // 2
    width = 2 * low_all.shape[3] // 2

    loads = [
        pltpu.make_async_copy(src, dst, load_sem.at[i])
        for i, (src, dst) in enumerate(
            [
                (feats_h, feats), (pre_h, pre), (down_h, down), (angle_h, angle),
                (up_h.at[0], up_all.at[mine]), (first_h, first), (second_h, second),
            ]
        )
    ]
    for load in loads[:3]:
        load.start()

    barrier = pltpu.get_barrier_semaphore()

    def greet(k, carry):
        pl.semaphore_signal(
            barrier, inc=1, device_id=(lax.rem(me + k, n), mine), device_id_type=MESH
        )
        return carry

    lax.fori_loop(1, n, greet, 0)
    for k in range(1, groups):
        pl.semaphore_signal(
            barrier, inc=1, device_id=(me, lax.rem(mine + k, groups)), device_id_type=MESH
        )

    def send(src, dst, ss, rs, to, to_basis):
        return pltpu.make_async_remote_copy(
            src_ref=src, dst_ref=dst, send_sem=ss, recv_sem=rs,
            device_id=(to, to_basis), device_id_type=MESH,
        )

    def meta_copy(d, slot):
        return send(meta.at[d], meta_recv.at[slot], meta_ss.at[d], meta_rs.at[slot], d, mine)

    def goal_copy(q, slot):
        return send(
            goals.at[q], goals_recv.at[slot], goal_ss.at[q], goal_rs.at[slot],
            layer * inner + q, mine,
        )

    def part_copy(h, q, slot):
        return send(
            part_send.at[h, q], part_recv.at[h, slot], part_ss.at[h, q], part_rs.at[h, slot],
            layer * inner + q, mine,
        )

    def plane_copy(h, z, slot):
        return send(
            plane_send.at[h, z], plane_recv.at[h, slot], plane_ss.at[h, z],
            plane_rs.at[h, slot], z * inner + spot, mine,
        )

    def atom_copy(d, slot):
        return send(
            atom_send.at[d], atom_recv.at[slot], atom_ss.at[d], atom_rs.at[slot], d, mine
        )

    def up_copy(g, slot):
        return send(up_h.at[0], up_all.at[slot], up_ss.at[g], up_rs.at[slot], me, g)

    def low_copy(g, slot):
        return send(low_all.at[mine], low_all.at[slot], low_ss.at[g], low_rs.at[slot], me, g)

    def pair_copy(h, g, slot):
        return send(
            paired.at[h, g], pair_recv.at[h, slot], pair_ss.at[h, g], pair_rs.at[h, slot], me, g
        )

    loads[0].wait()
    loads[1].wait()
    for load in loads[3:]:
        load.start()
    projected = silu(dot(feats[...], pre[...])).astype(bf16)
    loads[2].wait()
    down_twice = jnp.concatenate([down[...], down[...]], axis=0)
    lowered = silu(
        lax.dot_general(
            projected, down_twice, (((1,), (1,)), ((), ())), preferred_element_type=f32
        )
    ).reshape(nb, 2, half, width)
    lane = lax.broadcasted_iota(jnp.int32, (nb, half, width), 2)
    low_all[mine] = jnp.where(lane < width // 2, lowered[:, 0], lowered[:, 1]).astype(bf16)

    pl.semaphore_wait(barrier, n - 1 + groups - 1)
    others = [lax.rem(mine + k, groups) for k in range(1, groups)]
    for g in others:
        low_copy(g, mine).start()
    for g in others:
        up_copy(g, mine).start()

    parts = part_owner.shape[1]
    owner = part_owner[...]
    owner = (owner & (inner - 1)) * outer + (owner >> (inner.bit_length() - 1))
    owner_col, rank_row, rank_col = ranks(owner)
    match = lines((n * seat, parts), 0) == owner * seat + rank_row
    goal = jnp.sum(
        jnp.where(match, part_target[...] + 1, 0), axis=1, keepdims=True
    )
    spread_goal = jnp.broadcast_to(goal - 1, (n * seat, 128))
    goals[...] = spread_goal.reshape(inner, outer, seat, 128)
    match = lines((parts, n * seat), 1) == owner_col * seat + rank_col
    items_v[...] = jnp.sum(
        jnp.where(match, lines((parts, n * seat), 0), 0), axis=0, keepdims=True
    )
    item_copy = pltpu.make_async_copy(items_v, items, item_sem.at[0])
    item_copy.start()

    slots = slot_owner.shape[1]
    owner = slot_owner[...]
    owner_col, rank_row, rank_col = ranks(owner)
    match = lines((n * acap, slots), 0) == owner * acap + rank_row
    held = jnp.sum(
        jnp.where(match, lines((n * acap, slots), 1) + 1, 0), axis=1, keepdims=True
    )
    pick[...] = (held - 1 == edge_slot[...]).astype(f32).astype(bf16)
    wanted = jnp.where(
        lines((n, slots), 0) == owner, slot_atom[...].astype(f32) + 1.0, 0.0
    ).astype(bf16)
    first_lane = me * acap
    lanes = (lines((slots, n * acap), 1) == rank_col + first_lane).astype(f32).astype(bf16)
    atom_meta = dot(wanted, lanes).astype(jnp.int32)
    for r in range(chunks):
        meta[:, r, :] = atom_meta[:, r * 128 : (r + 1) * 128]

    spots = [lax.rem(spot + k, inner) for k in far_first(inner)]
    layers = [lax.rem(layer + k, outer) for k in far_first(outer)]
    for q in spots:
        goal_copy(q, spot).start()
    goals_recv[spot] = goals[spot]

    def start_meta(k, carry):
        meta_copy(lax.rem(me + k, n), me).start()
        return carry

    lax.fori_loop(1, n, start_meta, 0)
    meta_recv[me] = meta[me]

    def spread(g):
        lane = lax.broadcasted_iota(jnp.int32, (half, width), 1)
        left = lane < width // 2
        for i in range(nb):
            packed = low_all[g, i].astype(f32)
            turned = pltpu.roll(packed, width // 2, 1)
            at = g * nb + i
            diag[at, 0:half] = jnp.where(left, packed, 0.0).astype(bf16)
            diag[at, half : 2 * half] = jnp.where(left, turned, 0.0).astype(bf16)
            diag[at, 2 * half : 3 * half] = jnp.where(left, 0.0, turned).astype(bf16)
            diag[at, 3 * half :] = jnp.where(left, 0.0, packed).astype(bf16)

    spread(mine)
    loads[3].wait()
    for g in others:
        low_copy(g, g).wait_recv()
        spread(g)

    for p in range(parts):
        tile = angle[p, 0]
        wide = jnp.concatenate([tile[:half], tile[half:]], axis=1)
        prod[p] = dot(wide, diag[part_source[p]]).astype(bf16)
    item_copy.wait()

    pieces = part_send.shape[0]
    piece = half // pieces

    def fill(h, q, ref, slot):
        def fill_layer(z, carry):
            for s in range(cap):
                item = jnp.clip(items[0, (q * outer + z) * seat + s], 0, prod.shape[0] - 1)
                ref[h, slot, z, s] = prod[item, h * piece : (h + 1) * piece]
            return carry

        lax.fori_loop(0, outer, fill_layer, 0)

    for h in range(pieces):
        for q in spots:
            fill(h, q, part_send, q)
            part_copy(h, q, spot).start()
        fill(h, spot, part_recv, spot)

    loads[4].wait()
    for g in others:
        up_copy(g, g).wait_recv()
    blank = jnp.zeros(up_all.shape[1:], bf16)
    above = jnp.concatenate([x for g in range(groups) for x in (up_all[g], blank)], axis=0)
    below = jnp.concatenate([x for g in range(groups) for x in (blank, up_all[g])], axis=0)
    for load in loads[5:]:
        load.wait()

    depth = above.shape[1]
    for q in spots:
        goal_copy(q, q).wait_recv()

    def gather_layer(h):
        for q in spots:
            part_copy(h, q, q).wait_recv()

        def one(z, carry):
            pairs = [
                (goals_recv[q, z, s : s + 1, :], part_recv[h, q, z, s].astype(f32))
                for q in range(inner)
                for s in range(cap)
            ]
            for j in range(groups * nb):
                total = jnp.zeros((piece, width), f32)
                for t, a in pairs:
                    total = total + jnp.where(jnp.broadcast_to(t == j, a.shape), a, 0.0)
                plane_send[h, z, j] = total.astype(bf16)
            return carry

        lax.fori_loop(0, outer, one, 0)
        for z in layers:
            plane_copy(h, z, layer).start()
        plane_recv[h, layer] = plane_send[h, layer]

    def sum_layers(h):
        for z in layers:
            plane_copy(h, z, z).wait_recv()
        total = plane_recv[h, 0].astype(f32)
        for z in range(1, outer):
            total = total + plane_recv[h, z].astype(f32)
        paired[h] = total.astype(bf16).reshape(groups, nb * piece, width)
        for g in others:
            pair_copy(h, g, mine).start()
        pair_recv[h, mine] = paired[h, mine]

    def edge_layers(h):
        for g in others:
            pair_copy(h, g, g).wait_recv()
        columns = jnp.concatenate([pair_recv[h, g] for g in range(groups)], axis=1)
        upper = dot(columns, above).reshape(nb, 1, piece, depth)
        lower = dot(columns, below).reshape(nb, 1, piece, depth)
        triplet = jnp.concatenate([upper, lower], axis=1).reshape(2 * nb * piece, depth)
        starts = [q * half + h * piece for q in range(2 * nb)]
        own = jnp.concatenate([feats[at : at + piece] for at in starts], axis=0)
        joined = (own.astype(f32) + triplet).astype(bf16)
        inner = silu(dot(joined, first[...])).astype(bf16)
        deep = silu(dot(inner, second[...]))
        update = ((joined.astype(f32) + deep) * half_root).astype(bf16)
        for q, at in enumerate(starts):
            edge_out[at : at + piece] = update[q * piece : (q + 1) * piece]

    for h in range(pieces + 3):
        if h < pieces:
            gather_layer(h)
        if 0 <= h - 2 < pieces:
            sum_layers(h - 2)
        if 0 <= h - 3 < pieces:
            edge_layers(h - 3)

    edge_copy = pltpu.make_async_copy(edge_out, edge_h, edge_sem.at[0])
    edge_copy.start()
    atom_send[...] = dot(pick[...], edge_out[...]).astype(bf16).reshape(atom_send.shape)

    def start_atom(i, carry):
        for k in (n // 2 + i, n // 2 - i):
            atom_copy(lax.rem(me + k, n), me).start()
        return carry

    atom_copy(lax.rem(me + n // 2, n), me).start()
    lax.fori_loop(1, n // 2, start_atom, 0)
    atom_recv[me] = atom_send[me]

    def take_meta(i, carry):
        src = lax.rem(me + i, n)
        meta_copy(src, src).wait_recv()
        return carry

    lax.fori_loop(1, n, take_meta, 0)
    named = jnp.sum(meta_recv[...], axis=0)
    atoms = gathered.shape[0]
    ids = lines((atoms, 128), 0) + 1
    chosen = jnp.concatenate(
        [(ids == named[r : r + 1]).astype(f32).astype(bf16) for r in range(chunks)], axis=1
    )

    def take_atom(i, carry):
        src = lax.rem(me + i, n)
        atom_copy(src, src).wait_recv()
        return carry

    lax.fori_loop(1, n, take_atom, 0)
    gathered[...] = dot(
        chosen, atom_recv[...].reshape(n * acap, atom_recv.shape[2])
    ).astype(bf16)
    edge_copy.wait()

    def finish(k, carry):
        d = lax.rem(me + k, n)
        meta_copy(d, me).wait_send()
        atom_copy(d, me).wait_send()
        return carry

    lax.fori_loop(1, n, finish, 0)
    for q in spots:
        goal_copy(q, spot).wait_send()
        for h in range(pieces):
            part_copy(h, q, spot).wait_send()
    for z in layers:
        for h in range(pieces):
            plane_copy(h, z, layer).wait_send()
    for g in others:
        low_copy(g, mine).wait_send()
        up_copy(g, mine).wait_send()
        for h in range(pieces):
            pair_copy(h, g, mine).wait_send()


def atom_layers(
    edge_h, gathered, feats_h, first_h, second_h, edge_out, atom_out,
    edge, feats, first, second, load_sem, in_sem, out_sem,
):
    loads = [
        pltpu.make_async_copy(src, dst, load_sem.at[i])
        for i, (src, dst) in enumerate([(first_h, first), (second_h, second), (feats_h, feats)])
    ]
    share = edge.shape[0] // 4
    strips = [pl.ds(i * share, share) for i in range(4)]
    ins = [
        pltpu.make_async_copy(edge_h.at[at], edge.at[at], in_sem.at[i])
        for i, at in enumerate(strips)
    ]
    outs = [
        pltpu.make_async_copy(edge.at[at], edge_out.at[at], out_sem.at[i])
        for i, at in enumerate(strips)
    ]
    for copy in ins + loads:
        copy.start()
    for arrive, leave in zip(ins, outs):
        arrive.wait()
        leave.start()
    for load in loads:
        load.wait()
    hidden = silu(dot(gathered[...], first[...])).astype(bf16)
    atom_out[...] = (feats[...].astype(f32) + dot(hidden, second[...])).astype(bf16)
    for leave in outs:
        leave.wait()


def body(
    edge_feats, pre_weight, down_weight, angle_tiles, part_source, part_owner, part_target,
    up_weight, res_first, res_second, edge_slot, slot_owner, slot_atom, atom_feats,
    atom_first, atom_second,
):
    n, groups = lax.axis_size("graph"), lax.axis_size("basis")
    parts, _, block, _ = angle_tiles.shape
    narrow = down_weight.shape[1]
    rows, wide = edge_feats.shape
    nb = rows // block
    slot_count = slot_owner.shape[1]
    cap = max(2, 2 * parts // n)
    acap = -(-max(2, 2 * slot_count // n) // 16) * 16

    seat = -(-cap // 8) * 8
    chunks = n * acap // 128
    meta_rows = -(-chunks // 8) * 8
    pieces = min(4, block // 32)
    inner = 1
    while n % (2 * inner) == 0 and inner * inner < n:
        inner *= 2
    outer = n // inner
    piece = block // 2 // pieces

    half, pair_width = block // 2, 2 * narrow
    dma = pltpu.SemaphoreType.DMA
    vmem = pl.BlockSpec(memory_space=pltpu.VMEM)
    hbm = pl.BlockSpec(memory_space=pl.ANY)
    scratch = [
        pltpu.VMEM(edge_feats.shape, bf16),
        pltpu.VMEM(edge_feats.shape, bf16),
        pltpu.VMEM(pre_weight.shape, bf16),
        pltpu.VMEM(down_weight.shape[::-1], bf16),
        pltpu.VMEM(angle_tiles.shape, bf16),
        pltpu.VMEM((groups,) + up_weight.shape[1:], bf16),
        pltpu.VMEM(res_first.shape, bf16),
        pltpu.VMEM(res_second.shape, bf16),
        pltpu.VMEM((groups, nb, half, pair_width), bf16),
        pltpu.VMEM((groups * nb, 2 * block, pair_width), bf16),
        pltpu.VMEM((parts, half, pair_width), bf16),
        pltpu.VMEM((pieces, inner, outer, cap, piece, pair_width), bf16),
        pltpu.VMEM((pieces, inner, outer, cap, piece, pair_width), bf16),
        pltpu.VMEM((inner, outer, seat, 128), jnp.int32),
        pltpu.VMEM((inner, outer, seat, 128), jnp.int32),
        pltpu.VMEM((n, meta_rows, 128), jnp.int32),
        pltpu.VMEM((n, meta_rows, 128), jnp.int32),
        pltpu.VMEM((1, n * seat), jnp.int32),
        pltpu.SMEM((1, n * seat), jnp.int32),
        pltpu.VMEM((pieces, outer, groups * nb, piece, pair_width), bf16),
        pltpu.VMEM((pieces, outer, groups * nb, piece, pair_width), bf16),
        pltpu.VMEM((pieces, groups, nb * piece, pair_width), bf16),
        pltpu.VMEM((pieces, groups, nb * piece, pair_width), bf16),
        pltpu.VMEM((n * acap, rows), bf16),
        pltpu.VMEM((n, acap, wide), bf16),
        pltpu.VMEM((n, acap, wide), bf16),
        dma((7,)),
        dma((1,)),
        dma((1,)),
    ]
    scratch += [dma((inner,))] * 2 + [dma((n,))] * 2 + [dma((pieces, inner))] * 2
    scratch += [dma((pieces, outer))] * 2 + [dma((n,))] * 2
    scratch += [dma((groups,))] * 4 + [dma((pieces, groups))] * 2
    shapes = (
        jax.ShapeDtypeStruct(edge_feats.shape, bf16),
        jax.ShapeDtypeStruct(atom_feats.shape, bf16),
    )
    edge_update, gathered = pl.pallas_call(
        functools.partial(kernel, n, inner, groups, cap, acap, seat, chunks, nb, block),
        out_shape=shapes,
        in_specs=[pl.BlockSpec(memory_space=pltpu.SMEM)] + [vmem] * 5 + [hbm] * 7,
        out_specs=(hbm, vmem),
        scratch_shapes=scratch,
        compiler_params=pltpu.CompilerParams(
            collective_id=0, has_side_effects=True, vmem_limit_bytes=62 * 2**20
        ),
    )(
        part_source, part_owner.reshape(1, parts), part_target.reshape(1, parts),
        slot_owner.reshape(1, slot_count), slot_atom, edge_slot,
        edge_feats, pre_weight, down_weight.T,
        angle_tiles, up_weight, res_first, res_second,
    )
    return pl.pallas_call(
        atom_layers,
        out_shape=shapes,
        in_specs=[hbm, vmem, hbm, hbm, hbm],
        out_specs=(hbm, vmem),
        scratch_shapes=[
            pltpu.VMEM(edge_feats.shape, bf16),
            pltpu.VMEM(atom_feats.shape, bf16),
            pltpu.VMEM(atom_first.shape, bf16),
            pltpu.VMEM(atom_second.shape, bf16),
            dma((3,)),
            dma((4,)),
            dma((4,)),
        ],
        compiler_params=pltpu.CompilerParams(vmem_limit_bytes=62 * 2**20),
    )(edge_update, gathered, atom_feats, atom_first, atom_second)


def solution(mesh):
    rows = P(("graph", "basis"), None)
    in_specs = (
        rows,
        P(),
        P(),
        P("graph", "basis", None, None),
        P("graph"),
        P("graph", None),
        P("graph"),
        P("basis", None, None),
        P(),
        P(),
        rows,
        P(("graph", "basis"), None, None),
        rows,
        rows,
        P(),
        P(),
    )
    return jax.shard_map(
        body, mesh=mesh, in_specs=in_specs, out_specs=(rows, rows), check_vma=False
    )
```

```python
import functools

import jax
import jax.numpy as jnp
from jax import lax
from jax.experimental import pallas as pl
from jax.experimental.pallas import tpu as pltpu
from jax.sharding import PartitionSpec as P

half_root = 0.5**0.5
MESH = pl.DeviceIdType.MESH
bf16 = jnp.bfloat16
f32 = jnp.float32


def dot(a, b):
    return jnp.dot(a, b, preferred_element_type=f32)


def silu(v):
    w = 0.5 * v
    return w + w * jnp.tanh(w)


def lines(shape, axis):
    return lax.broadcasted_iota(jnp.int32, shape, axis)


def far_first(count):
    return sorted(range(1, count), key=lambda k: abs(2 * k - count))


def ranks(row):
    count = row.shape[1]
    down, along = lines((count, count), 0), lines((count, count), 1)
    col = jnp.sum(jnp.where(down == along, row, 0), axis=1, keepdims=True)
    same = jnp.where(col == row, 1, 0)
    rank_row = jnp.sum(jnp.where(down < along, same, 0), axis=0, keepdims=True)
    rank_col = jnp.sum(jnp.where(along < down, same, 0), axis=1, keepdims=True)
    return col, rank_row, rank_col


def kernel(
    n, inner, groups, cap, acap, seat, chunks, nb, block,
    source_h, owner_h, target_h, slot_owner_h, slot_atom_h, edge_slot_h,
    feats_h, pre_h, down_h, angle_h, up_h, first_h, second_h,
    edge_h, gathered,
    part_source, part_owner, part_target, slot_owner, slot_atom, edge_slot,
    edge_out,
    feats, pre, down, angle, up_all, first, second,
    low_all, diag, prod, part_send, part_recv, goals, goals_recv, meta, meta_recv, items_v, items,
    plane_send, plane_recv, paired, pair_recv, pick, atom_send, atom_recv,
    load_sem, small_sem, item_sem, edge_sem, goal_ss, goal_rs, meta_ss, meta_rs, part_ss, part_rs, plane_ss, plane_rs, atom_ss, atom_rs,
    low_ss, low_rs, up_ss, up_rs, pair_ss, pair_rs,
):
    me = lax.axis_index("graph")
    mine = lax.axis_index("basis")
    outer = n // inner
    layer, spot = me // inner, lax.rem(me, inner)
    half = block // 2
    width = 2 * low_all.shape[3] // 2

    loads = [
        pltpu.make_async_copy(src, dst, load_sem.at[i])
        for i, (src, dst) in enumerate(
            [
                (feats_h, feats), (pre_h, pre), (down_h, down), (angle_h, angle),
                (up_h.at[0], up_all.at[mine]), (first_h, first), (second_h, second),
            ]
        )
    ]
    small = [
        pltpu.make_async_copy(src, dst, small_sem.at[i])
        for i, (src, dst) in enumerate(
            [
                (source_h, part_source), (owner_h, part_owner), (target_h, part_target),
                (slot_owner_h, slot_owner), (slot_atom_h, slot_atom), (edge_slot_h, edge_slot),
            ]
        )
    ]
    for load in loads[:3] + small:
        load.start()

    barrier = pltpu.get_barrier_semaphore()

    def greet(k, carry):
        pl.semaphore_signal(
            barrier, inc=1, device_id=(lax.rem(me + k, n), mine), device_id_type=MESH
        )
        return carry

    lax.fori_loop(1, n, greet, 0)
    for k in range(1, groups):
        pl.semaphore_signal(
            barrier, inc=1, device_id=(me, lax.rem(mine + k, groups)), device_id_type=MESH
        )

    def send(src, dst, ss, rs, to, to_basis):
        return pltpu.make_async_remote_copy(
            src_ref=src, dst_ref=dst, send_sem=ss, recv_sem=rs,
            device_id=(to, to_basis), device_id_type=MESH,
        )

    def meta_copy(d, slot):
        return send(meta.at[d], meta_recv.at[slot], meta_ss.at[d], meta_rs.at[slot], d, mine)

    def goal_copy(q, slot):
        return send(
            goals.at[q], goals_recv.at[slot], goal_ss.at[q], goal_rs.at[slot],
            layer * inner + q, mine,
        )

    def part_copy(h, q, slot):
        return send(
            part_send.at[h, q], part_recv.at[h, slot], part_ss.at[h, q], part_rs.at[h, slot],
            layer * inner + q, mine,
        )

    def plane_copy(h, z, slot):
        return send(
            plane_send.at[h, z], plane_recv.at[h, slot], plane_ss.at[h, z],
            plane_rs.at[h, slot], z * inner + spot, mine,
        )

    def atom_copy(d, slot):
        return send(
            atom_send.at[d], atom_recv.at[slot], atom_ss.at[d], atom_rs.at[slot], d, mine
        )

    def up_copy(g, slot):
        return send(up_h.at[0], up_all.at[slot], up_ss.at[g], up_rs.at[slot], me, g)

    def low_copy(g, slot):
        return send(low_all.at[mine], low_all.at[slot], low_ss.at[g], low_rs.at[slot], me, g)

    def pair_copy(h, g, slot):
        return send(
            paired.at[h, g], pair_recv.at[h, slot], pair_ss.at[h, g], pair_rs.at[h, slot], me, g
        )

    loads[0].wait()
    loads[1].wait()
    for load in loads[3:]:
        load.start()
    projected = silu(dot(feats[...], pre[...])).astype(bf16)
    loads[2].wait()
    down_twice = jnp.concatenate([down[...], down[...]], axis=0)
    lowered = silu(
        lax.dot_general(
            projected, down_twice, (((1,), (1,)), ((), ())), preferred_element_type=f32
        )
    ).reshape(nb, 2, half, width)
    lane = lax.broadcasted_iota(jnp.int32, (nb, half, width), 2)
    low_all[mine] = jnp.where(lane < width // 2, lowered[:, 0], lowered[:, 1]).astype(bf16)

    pl.semaphore_wait(barrier, n - 1 + groups - 1)
    others = [lax.rem(mine + k, groups) for k in range(1, groups)]
    for g in others:
        low_copy(g, mine).start()
    for g in others:
        up_copy(g, mine).start()

    for load in small:
        load.wait()
    parts = part_owner.shape[1]
    owner = part_owner[...]
    owner = (owner & (inner - 1)) * outer + (owner >> (inner.bit_length() - 1))
    owner_col, rank_row, rank_col = ranks(owner)
    match = lines((n * seat, parts), 0) == owner * seat + rank_row
    goal = jnp.sum(
        jnp.where(match, part_target[...] + 1, 0), axis=1, keepdims=True
    )
    spread_goal = jnp.broadcast_to(goal - 1, (n * seat, 128))
    goals[...] = spread_goal.reshape(inner, outer, seat, 128)
    match = lines((parts, n * seat), 1) == owner_col * seat + rank_col
    items_v[...] = jnp.sum(
        jnp.where(match, lines((parts, n * seat), 0), 0), axis=0, keepdims=True
    )
    item_copy = pltpu.make_async_copy(items_v, items, item_sem.at[0])
    item_copy.start()

    spots = [lax.rem(spot + k, inner) for k in far_first(inner)]
    layers = [lax.rem(layer + k, outer) for k in far_first(outer)]
    for q in spots:
        goal_copy(q, spot).start()
    goals_recv[spot] = goals[spot]

    def spread(g):
        lane = lax.broadcasted_iota(jnp.int32, (half, width), 1)
        left = lane < width // 2
        for i in range(nb):
            packed = low_all[g, i].astype(f32)
            turned = pltpu.roll(packed, width // 2, 1)
            at = g * nb + i
            diag[at, 0:half] = jnp.where(left, packed, 0.0).astype(bf16)
            diag[at, half : 2 * half] = jnp.where(left, turned, 0.0).astype(bf16)
            diag[at, 2 * half : 3 * half] = jnp.where(left, 0.0, turned).astype(bf16)
            diag[at, 3 * half :] = jnp.where(left, 0.0, packed).astype(bf16)

    spread(mine)
    loads[3].wait()
    for g in others:
        low_copy(g, g).wait_recv()
        spread(g)

    for p in range(parts):
        tile = angle[p, 0]
        wide = jnp.concatenate([tile[:half], tile[half:]], axis=1)
        prod[p] = dot(wide, diag[jnp.clip(part_source[p], 0, groups * nb - 1)]).astype(bf16)
    item_copy.wait()

    pieces = part_send.shape[0]
    piece = half // pieces

    def fill(h, q, ref, slot):
        def fill_layer(z, carry):
            for s in range(cap):
                item = jnp.clip(items[0, (q * outer + z) * seat + s], 0, prod.shape[0] - 1)
                ref[h, slot, z, s] = prod[item, h * piece : (h + 1) * piece]
            return carry

        lax.fori_loop(0, outer, fill_layer, 0)

    for h in range(pieces):
        for q in spots:
            fill(h, q, part_send, q)
            part_copy(h, q, spot).start()
        fill(h, spot, part_recv, spot)

    slots = slot_owner.shape[1]
    owner = slot_owner[...]
    owner_col, rank_row, rank_col = ranks(owner)
    match = lines((n * acap, slots), 0) == owner * acap + rank_row
    held = jnp.sum(
        jnp.where(match, lines((n * acap, slots), 1) + 1, 0), axis=1, keepdims=True
    )
    pick[...] = (held - 1 == edge_slot[...]).astype(f32).astype(bf16)
    wanted = jnp.where(
        lines((n, slots), 0) == owner, slot_atom[...].astype(f32) + 1.0, 0.0
    ).astype(bf16)
    first_lane = me * acap
    lanes = (lines((slots, n * acap), 1) == rank_col + first_lane).astype(f32).astype(bf16)
    atom_meta = dot(wanted, lanes).astype(jnp.int32)
    for r in range(chunks):
        meta[:, r, :] = atom_meta[:, r * 128 : (r + 1) * 128]

    def start_meta(k, carry):
        meta_copy(lax.rem(me + k, n), me).start()
        return carry

    lax.fori_loop(1, n, start_meta, 0)
    meta_recv[me] = meta[me]

    loads[4].wait()
    for g in others:
        up_copy(g, g).wait_recv()
    blank = jnp.zeros(up_all.shape[1:], bf16)
    above = jnp.concatenate([x for g in range(groups) for x in (up_all[g], blank)], axis=0)
    below = jnp.concatenate([x for g in range(groups) for x in (blank, up_all[g])], axis=0)
    for load in loads[5:]:
        load.wait()

    depth = above.shape[1]
    for q in spots:
        goal_copy(q, q).wait_recv()

    def gather_layer(h):
        for q in spots:
            part_copy(h, q, q).wait_recv()

        def one(z, carry):
            pairs = [
                (goals_recv[q, z, s : s + 1, :], part_recv[h, q, z, s].astype(f32))
                for q in range(inner)
                for s in range(cap)
            ]
            for j in range(groups * nb):
                total = jnp.zeros((piece, width), f32)
                for t, a in pairs:
                    total = total + jnp.where(jnp.broadcast_to(t == j, a.shape), a, 0.0)
                plane_send[h, z, j] = total.astype(bf16)
            return carry

        lax.fori_loop(0, outer, one, 0)
        for z in layers:
            plane_copy(h, z, layer).start()
        plane_recv[h, layer] = plane_send[h, layer]

    def sum_layers(h):
        for z in layers:
            plane_copy(h, z, z).wait_recv()
        total = plane_recv[h, 0].astype(f32)
        for z in range(1, outer):
            total = total + plane_recv[h, z].astype(f32)
        paired[h] = total.astype(bf16).reshape(groups, nb * piece, width)
        for g in others:
            pair_copy(h, g, mine).start()
        pair_recv[h, mine] = paired[h, mine]

    def edge_layers(h):
        for g in others:
            pair_copy(h, g, g).wait_recv()
        columns = jnp.concatenate([pair_recv[h, g] for g in range(groups)], axis=1)
        upper = dot(columns, above).reshape(nb, 1, piece, depth)
        lower = dot(columns, below).reshape(nb, 1, piece, depth)
        triplet = jnp.concatenate([upper, lower], axis=1).reshape(2 * nb * piece, depth)
        starts = [q * half + h * piece for q in range(2 * nb)]
        own = jnp.concatenate([feats[at : at + piece] for at in starts], axis=0)
        joined = (own.astype(f32) + triplet).astype(bf16)
        inner = silu(dot(joined, first[...])).astype(bf16)
        deep = silu(dot(inner, second[...]))
        update = ((joined.astype(f32) + deep) * half_root).astype(bf16)
        for q, at in enumerate(starts):
            edge_out[at : at + piece] = update[q * piece : (q + 1) * piece]

    for h in range(pieces + 3):
        if h < pieces:
            gather_layer(h)
        if 0 <= h - 2 < pieces:
            sum_layers(h - 2)
        if 0 <= h - 3 < pieces:
            edge_layers(h - 3)

    edge_copy = pltpu.make_async_copy(edge_out, edge_h, edge_sem.at[0])
    edge_copy.start()
    atom_send[...] = dot(pick[...], edge_out[...]).astype(bf16).reshape(atom_send.shape)

    def start_atom(i, carry):
        for k in (n // 2 + i, n // 2 - i):
            atom_copy(lax.rem(me + k, n), me).start()
        return carry

    atom_copy(lax.rem(me + n // 2, n), me).start()
    lax.fori_loop(1, n // 2, start_atom, 0)
    atom_recv[me] = atom_send[me]

    def take_meta(i, carry):
        src = lax.rem(me + i, n)
        meta_copy(src, src).wait_recv()
        return carry

    lax.fori_loop(1, n, take_meta, 0)
    named = jnp.sum(meta_recv[...], axis=0)
    atoms = gathered.shape[0]
    ids = lines((atoms, 128), 0) + 1
    chosen = jnp.concatenate(
        [(ids == named[r : r + 1]).astype(f32).astype(bf16) for r in range(chunks)], axis=1
    )

    def take_atom(i, carry):
        src = lax.rem(me + i, n)
        atom_copy(src, src).wait_recv()
        return carry

    lax.fori_loop(1, n, take_atom, 0)
    gathered[...] = dot(
        chosen, atom_recv[...].reshape(n * acap, atom_recv.shape[2])
    ).astype(bf16)
    edge_copy.wait()

    def finish(k, carry):
        d = lax.rem(me + k, n)
        meta_copy(d, me).wait_send()
        atom_copy(d, me).wait_send()
        return carry

    lax.fori_loop(1, n, finish, 0)
    for q in spots:
        goal_copy(q, spot).wait_send()
        for h in range(pieces):
            part_copy(h, q, spot).wait_send()
    for z in layers:
        for h in range(pieces):
            plane_copy(h, z, layer).wait_send()
    for g in others:
        low_copy(g, mine).wait_send()
        up_copy(g, mine).wait_send()
        for h in range(pieces):
            pair_copy(h, g, mine).wait_send()


def atom_layers(
    edge_h, gathered_h, feats_h, first_h, second_h, edge_out, atom_h,
    edge, gathered, feats, first, second, atom_out, load_sem, in_sem, out_sem,
):
    loads = [
        pltpu.make_async_copy(src, dst, load_sem.at[i])
        for i, (src, dst) in enumerate(
            [(gathered_h, gathered), (first_h, first), (second_h, second), (feats_h, feats)]
        )
    ]
    share = edge.shape[0] // 4
    strips = [pl.ds(i * share, share) for i in range(4)]
    ins = [
        pltpu.make_async_copy(edge_h.at[at], edge.at[at], in_sem.at[i])
        for i, at in enumerate(strips)
    ]
    outs = [
        pltpu.make_async_copy(edge.at[at], edge_out.at[at], out_sem.at[i])
        for i, at in enumerate(strips)
    ]
    for copy in loads + ins:
        copy.start()
    for arrive, leave in zip(ins, outs):
        arrive.wait()
        leave.start()
    for load in loads:
        load.wait()
    hidden = silu(dot(gathered[...], first[...])).astype(bf16)
    atom_out[...] = (feats[...].astype(f32) + dot(hidden, second[...])).astype(bf16)
    outs.append(pltpu.make_async_copy(atom_out, atom_h, load_sem.at[4]))
    outs[-1].start()
    for leave in outs:
        leave.wait()


def body(
    edge_feats, pre_weight, down_weight, angle_tiles, part_source, part_owner, part_target,
    up_weight, res_first, res_second, edge_slot, slot_owner, slot_atom, atom_feats,
    atom_first, atom_second,
):
    n, groups = lax.axis_size("graph"), lax.axis_size("basis")
    parts, _, block, _ = angle_tiles.shape
    narrow = down_weight.shape[1]
    rows, wide = edge_feats.shape
    nb = rows // block
    slot_count = slot_owner.shape[1]
    cap = max(2, 2 * parts // n)
    acap = -(-max(2, 2 * slot_count // n) // 16) * 16

    seat = -(-cap // 8) * 8
    chunks = n * acap // 128
    meta_rows = -(-chunks // 8) * 8
    pieces = min(4, block // 32)
    inner = 1
    while n % (2 * inner) == 0 and inner * inner < n:
        inner *= 2
    outer = n // inner
    piece = block // 2 // pieces

    half, pair_width = block // 2, 2 * narrow
    dma = pltpu.SemaphoreType.DMA
    vmem = pl.BlockSpec(memory_space=pltpu.VMEM)
    hbm = pl.BlockSpec(memory_space=pl.ANY)
    scratch = [
        pltpu.SMEM((parts,), jnp.int32),
        pltpu.VMEM((1, parts), jnp.int32),
        pltpu.VMEM((1, parts), jnp.int32),
        pltpu.VMEM((1, slot_count), jnp.int32),
        pltpu.VMEM((1, slot_count), jnp.int32),
        pltpu.VMEM((1, rows), jnp.int32),
        pltpu.VMEM(edge_feats.shape, bf16),
        pltpu.VMEM(edge_feats.shape, bf16),
        pltpu.VMEM(pre_weight.shape, bf16),
        pltpu.VMEM(down_weight.shape[::-1], bf16),
        pltpu.VMEM(angle_tiles.shape, bf16),
        pltpu.VMEM((groups,) + up_weight.shape[1:], bf16),
        pltpu.VMEM(res_first.shape, bf16),
        pltpu.VMEM(res_second.shape, bf16),
        pltpu.VMEM((groups, nb, half, pair_width), bf16),
        pltpu.VMEM((groups * nb, 2 * block, pair_width), bf16),
        pltpu.VMEM((parts, half, pair_width), bf16),
        pltpu.VMEM((pieces, inner, outer, cap, piece, pair_width), bf16),
        pltpu.VMEM((pieces, inner, outer, cap, piece, pair_width), bf16),
        pltpu.VMEM((inner, outer, seat, 128), jnp.int32),
        pltpu.VMEM((inner, outer, seat, 128), jnp.int32),
        pltpu.VMEM((n, meta_rows, 128), jnp.int32),
        pltpu.VMEM((n, meta_rows, 128), jnp.int32),
        pltpu.VMEM((1, n * seat), jnp.int32),
        pltpu.SMEM((1, n * seat), jnp.int32),
        pltpu.VMEM((pieces, outer, groups * nb, piece, pair_width), bf16),
        pltpu.VMEM((pieces, outer, groups * nb, piece, pair_width), bf16),
        pltpu.VMEM((pieces, groups, nb * piece, pair_width), bf16),
        pltpu.VMEM((pieces, groups, nb * piece, pair_width), bf16),
        pltpu.VMEM((n * acap, rows), bf16),
        pltpu.VMEM((n, acap, wide), bf16),
        pltpu.VMEM((n, acap, wide), bf16),
        dma((7,)),
        dma((6,)),
        dma((1,)),
        dma((1,)),
    ]
    scratch += [dma((inner,))] * 2 + [dma((n,))] * 2 + [dma((pieces, inner))] * 2
    scratch += [dma((pieces, outer))] * 2 + [dma((n,))] * 2
    scratch += [dma((groups,))] * 4 + [dma((pieces, groups))] * 2
    shapes = (
        jax.ShapeDtypeStruct(edge_feats.shape, bf16),
        jax.ShapeDtypeStruct(atom_feats.shape, bf16),
    )
    edge_update, gathered = pl.pallas_call(
        functools.partial(kernel, n, inner, groups, cap, acap, seat, chunks, nb, block),
        out_shape=shapes,
        in_specs=[hbm] * 13,
        out_specs=(hbm, vmem),
        scratch_shapes=scratch,
        compiler_params=pltpu.CompilerParams(
            collective_id=0, has_side_effects=True, vmem_limit_bytes=62 * 2**20
        ),
    )(
        part_source, part_owner.reshape(1, parts), part_target.reshape(1, parts),
        slot_owner.reshape(1, slot_count), slot_atom, edge_slot,
        edge_feats, pre_weight, down_weight.T,
        angle_tiles, up_weight, res_first, res_second,
    )
    return pl.pallas_call(
        atom_layers,
        out_shape=shapes,
        in_specs=[hbm] * 5,
        out_specs=(hbm, hbm),
        scratch_shapes=[
            pltpu.VMEM(edge_feats.shape, bf16),
            pltpu.VMEM(atom_feats.shape, bf16),
            pltpu.VMEM(atom_feats.shape, bf16),
            pltpu.VMEM(atom_first.shape, bf16),
            pltpu.VMEM(atom_second.shape, bf16),
            pltpu.VMEM(atom_feats.shape, bf16),
            dma((5,)),
            dma((4,)),
            dma((4,)),
        ],
        compiler_params=pltpu.CompilerParams(vmem_limit_bytes=62 * 2**20),
    )(edge_update, gathered, atom_feats, atom_first, atom_second)


def solution(mesh):
    rows = P(("graph", "basis"), None)
    in_specs = (
        rows,
        P(),
        P(),
        P("graph", "basis", None, None),
        P("graph"),
        P("graph", None),
        P("graph"),
        P("basis", None, None),
        P(),
        P(),
        rows,
        P(("graph", "basis"), None, None),
        rows,
        rows,
        P(),
        P(),
    )
    return jax.shard_map(
        body, mesh=mesh, in_specs=in_specs, out_specs=(rows, rows), check_vma=False
    )
```

```python
import functools

import jax
import jax.numpy as jnp
from jax import lax
from jax.experimental import pallas as pl
from jax.experimental.pallas import tpu as pltpu
from jax.sharding import PartitionSpec as P

half_root = 0.5**0.5
MESH = pl.DeviceIdType.MESH
bf16 = jnp.bfloat16
f32 = jnp.float32


def dot(a, b):
    return jnp.dot(a, b, preferred_element_type=f32)


def silu(v):
    w = 0.5 * v
    return w + w * jnp.tanh(w)


def lines(shape, axis):
    return lax.broadcasted_iota(jnp.int32, shape, axis)


def far_first(count):
    return sorted(range(1, count), key=lambda k: abs(2 * k - count))


def ranks(row):
    count = row.shape[1]
    down, along = lines((count, count), 0), lines((count, count), 1)
    col = jnp.sum(jnp.where(down == along, row, 0), axis=1, keepdims=True)
    same = jnp.where(col == row, 1, 0)
    rank_row = jnp.sum(jnp.where(down < along, same, 0), axis=0, keepdims=True)
    rank_col = jnp.sum(jnp.where(along < down, same, 0), axis=1, keepdims=True)
    return col, rank_row, rank_col


def kernel(
    n, inner, groups, cap, acap, seat, chunks, nb, block,
    source_h, owner_h, target_h, slot_owner_h, slot_atom_h, edge_slot_h,
    feats_h, pre_h, down_h, angle_h, up_h, first_h, second_h,
    edge_h, gathered,
    part_source, part_owner, part_target, slot_owner, slot_atom, edge_slot,
    edge_out,
    feats, pre, down, angle, up_all, first, second,
    low_all, diag, prod, part_send, part_recv, goals, goals_recv, meta, meta_recv, items_v, items,
    plane_send, plane_recv, paired, pair_recv, pick, atom_send, atom_recv,
    load_sem, small_sem, item_sem, edge_sem, goal_ss, goal_rs, meta_ss, meta_rs, part_ss, part_rs, plane_ss, plane_rs, atom_ss, atom_rs,
    low_ss, low_rs, up_ss, up_rs, pair_ss, pair_rs,
):
    me = lax.axis_index("graph")
    mine = lax.axis_index("basis")
    outer = n // inner
    layer, spot = me // inner, lax.rem(me, inner)
    half = block // 2
    width = 2 * low_all.shape[3] // 2

    loads = [
        pltpu.make_async_copy(src, dst, load_sem.at[i])
        for i, (src, dst) in enumerate(
            [
                (feats_h, feats), (pre_h, pre), (down_h, down), (angle_h, angle),
                (up_h.at[0], up_all.at[mine]), (first_h, first), (second_h, second),
            ]
        )
    ]
    small = [
        pltpu.make_async_copy(src, dst, small_sem.at[i])
        for i, (src, dst) in enumerate(
            [
                (source_h, part_source), (owner_h, part_owner), (target_h, part_target),
                (slot_owner_h, slot_owner), (slot_atom_h, slot_atom), (edge_slot_h, edge_slot),
            ]
        )
    ]
    for load in loads[:3] + small:
        load.start()

    barrier = pltpu.get_barrier_semaphore()

    def greet(k, carry):
        pl.semaphore_signal(
            barrier, inc=1, device_id=(lax.rem(me + k, n), mine), device_id_type=MESH
        )
        return carry

    lax.fori_loop(1, n, greet, 0)
    for k in range(1, groups):
        pl.semaphore_signal(
            barrier, inc=1, device_id=(me, lax.rem(mine + k, groups)), device_id_type=MESH
        )

    def send(src, dst, ss, rs, to, to_basis):
        return pltpu.make_async_remote_copy(
            src_ref=src, dst_ref=dst, send_sem=ss, recv_sem=rs,
            device_id=(to, to_basis), device_id_type=MESH,
        )

    def meta_copy(d, slot):
        return send(meta.at[d], meta_recv.at[slot], meta_ss.at[d], meta_rs.at[slot], d, mine)

    def goal_copy(q, slot):
        return send(
            goals.at[q], goals_recv.at[slot], goal_ss.at[q], goal_rs.at[slot],
            layer * inner + q, mine,
        )

    def part_copy(h, q, slot):
        return send(
            part_send.at[h, q], part_recv.at[h, slot], part_ss.at[h, q], part_rs.at[h, slot],
            layer * inner + q, mine,
        )

    def plane_copy(h, z, slot):
        return send(
            plane_send.at[h, z], plane_recv.at[h, slot], plane_ss.at[h, z],
            plane_rs.at[h, slot], z * inner + spot, mine,
        )

    def atom_copy(d, slot):
        return send(
            atom_send.at[d], atom_recv.at[slot], atom_ss.at[d], atom_rs.at[slot], d, mine
        )

    def up_copy(g, slot):
        return send(up_h.at[0], up_all.at[slot], up_ss.at[g], up_rs.at[slot], me, g)

    def low_copy(g, slot):
        return send(low_all.at[mine], low_all.at[slot], low_ss.at[g], low_rs.at[slot], me, g)

    def pair_copy(h, g, slot):
        return send(
            paired.at[h, g], pair_recv.at[h, slot], pair_ss.at[h, g], pair_rs.at[h, slot], me, g
        )

    loads[0].wait()
    loads[1].wait()
    for load in loads[3:]:
        load.start()
    projected = silu(dot(feats[...], pre[...])).astype(bf16)
    loads[2].wait()
    down_twice = jnp.concatenate([down[...], down[...]], axis=0)
    lowered = silu(
        lax.dot_general(
            projected, down_twice, (((1,), (1,)), ((), ())), preferred_element_type=f32
        )
    ).reshape(nb, 2, half, width)
    lane = lax.broadcasted_iota(jnp.int32, (nb, half, width), 2)
    low_all[mine] = jnp.where(lane < width // 2, lowered[:, 0], lowered[:, 1]).astype(bf16)

    pl.semaphore_wait(barrier, n - 1 + groups - 1)
    others = [lax.rem(mine + k, groups) for k in range(1, groups)]
    for g in others:
        low_copy(g, mine).start()
    for g in others:
        up_copy(g, mine).start()

    for load in small:
        load.wait()
    parts = part_owner.shape[1]
    owner = part_owner[...]
    owner = (owner & (inner - 1)) * outer + (owner >> (inner.bit_length() - 1))
    owner_col, rank_row, rank_col = ranks(owner)
    match = lines((n * seat, parts), 0) == owner * seat + rank_row
    goal = jnp.sum(
        jnp.where(match, part_target[...] + 1, 0), axis=1, keepdims=True
    )
    spread_goal = jnp.broadcast_to(goal - 1, (n * seat, 128))
    goals[...] = spread_goal.reshape(inner, outer, seat, 128)
    match = lines((parts, n * seat), 1) == owner_col * seat + rank_col
    items_v[...] = jnp.sum(
        jnp.where(match, lines((parts, n * seat), 0), 0), axis=0, keepdims=True
    )
    item_copy = pltpu.make_async_copy(items_v, items, item_sem.at[0])
    item_copy.start()

    spots = [lax.rem(spot + k, inner) for k in far_first(inner)]
    layers = [lax.rem(layer + k, outer) for k in far_first(outer)]
    for q in spots:
        goal_copy(q, spot).start()
    goals_recv[spot] = goals[spot]

    def spread(g):
        lane = lax.broadcasted_iota(jnp.int32, (half, width), 1)
        left = lane < width // 2
        for i in range(nb):
            packed = low_all[g, i].astype(f32)
            turned = pltpu.roll(packed, width // 2, 1)
            at = g * nb + i
            diag[at, 0:half] = jnp.where(left, packed, 0.0).astype(bf16)
            diag[at, half : 2 * half] = jnp.where(left, turned, 0.0).astype(bf16)
            diag[at, 2 * half : 3 * half] = jnp.where(left, 0.0, turned).astype(bf16)
            diag[at, 3 * half :] = jnp.where(left, 0.0, packed).astype(bf16)

    spread(mine)
    loads[3].wait()
    for g in others:
        low_copy(g, g).wait_recv()
        spread(g)

    for p in range(parts):
        tile = angle[p, 0]
        wide = jnp.concatenate([tile[:half], tile[half:]], axis=1)
        prod[p] = dot(wide, diag[jnp.clip(part_source[p], 0, groups * nb - 1)]).astype(bf16)
    item_copy.wait()

    pieces = part_send.shape[0]
    piece = half // pieces

    def fill(h, q, ref, slot):
        def fill_layer(z, carry):
            for s in range(cap):
                item = jnp.clip(items[0, (q * outer + z) * seat + s], 0, prod.shape[0] - 1)
                ref[h, slot, z, s] = prod[item, h * piece : (h + 1) * piece]
            return carry

        lax.fori_loop(0, outer, fill_layer, 0)

    for h in range(pieces):
        for q in spots:
            fill(h, q, part_send, q)
            part_copy(h, q, spot).start()
        fill(h, spot, part_recv, spot)

    slots = slot_owner.shape[1]
    owner = slot_owner[...]
    owner_col, rank_row, rank_col = ranks(owner)
    match = lines((n * acap, slots), 0) == owner * acap + rank_row
    held = jnp.sum(
        jnp.where(match, lines((n * acap, slots), 1) + 1, 0), axis=1, keepdims=True
    )
    pick[...] = (held - 1 == edge_slot[...]).astype(f32).astype(bf16)
    wanted = jnp.where(
        lines((n, slots), 0) == owner, slot_atom[...].astype(f32) + 1.0, 0.0
    ).astype(bf16)
    first_lane = me * acap
    lanes = (lines((slots, n * acap), 1) == rank_col + first_lane).astype(f32).astype(bf16)
    atom_meta = dot(wanted, lanes).astype(jnp.int32)
    for r in range(chunks):
        meta[:, r, :] = atom_meta[:, r * 128 : (r + 1) * 128]

    def start_meta(k, carry):
        meta_copy(lax.rem(me + k, n), me).start()
        return carry

    lax.fori_loop(1, n, start_meta, 0)
    meta_recv[me] = meta[me]

    loads[4].wait()
    for g in others:
        up_copy(g, g).wait_recv()
    blank = jnp.zeros(up_all.shape[1:], bf16)
    above = jnp.concatenate([x for g in range(groups) for x in (up_all[g], blank)], axis=0)
    below = jnp.concatenate([x for g in range(groups) for x in (blank, up_all[g])], axis=0)
    for load in loads[5:]:
        load.wait()

    depth = above.shape[1]
    for q in spots:
        goal_copy(q, q).wait_recv()

    def gather_layer(h):
        for q in spots:
            part_copy(h, q, q).wait_recv()

        def one(z, carry):
            pairs = [
                (goals_recv[q, z, s : s + 1, :], part_recv[h, q, z, s].astype(f32))
                for q in range(inner)
                for s in range(cap)
            ]
            for j in range(groups * nb):
                total = jnp.zeros((piece, width), f32)
                for t, a in pairs:
                    total = total + jnp.where(jnp.broadcast_to(t == j, a.shape), a, 0.0)
                plane_send[h, z, j] = total.astype(bf16)
            return carry

        lax.fori_loop(0, outer, one, 0)
        for z in layers:
            plane_copy(h, z, layer).start()
        plane_recv[h, layer] = plane_send[h, layer]

    def sum_layers(h):
        for z in layers:
            plane_copy(h, z, z).wait_recv()
        total = plane_recv[h, 0].astype(f32)
        for z in range(1, outer):
            total = total + plane_recv[h, z].astype(f32)
        paired[h] = total.astype(bf16).reshape(groups, nb * piece, width)
        for g in others:
            pair_copy(h, g, mine).start()
        pair_recv[h, mine] = paired[h, mine]

    def edge_layers(h):
        for g in others:
            pair_copy(h, g, g).wait_recv()
        columns = jnp.concatenate([pair_recv[h, g] for g in range(groups)], axis=1)
        upper = dot(columns, above).reshape(nb, 1, piece, depth)
        lower = dot(columns, below).reshape(nb, 1, piece, depth)
        triplet = jnp.concatenate([upper, lower], axis=1).reshape(2 * nb * piece, depth)
        starts = [q * half + h * piece for q in range(2 * nb)]
        own = jnp.concatenate([feats[at : at + piece] for at in starts], axis=0)
        joined = (own.astype(f32) + triplet).astype(bf16)
        inner = silu(dot(joined, first[...])).astype(bf16)
        deep = silu(dot(inner, second[...]))
        update = ((joined.astype(f32) + deep) * half_root).astype(bf16)
        for q, at in enumerate(starts):
            edge_out[at : at + piece] = update[q * piece : (q + 1) * piece]

    for h in range(pieces + 3):
        if h < pieces:
            gather_layer(h)
        if 0 <= h - 2 < pieces:
            sum_layers(h - 2)
        if 0 <= h - 3 < pieces:
            edge_layers(h - 3)

    edge_copy = pltpu.make_async_copy(edge_out, edge_h, edge_sem.at[0])
    edge_copy.start()
    atom_send[...] = dot(pick[...], edge_out[...]).astype(bf16).reshape(atom_send.shape)

    def start_atom(i, carry):
        for k in (n // 2 + i, n // 2 - i):
            atom_copy(lax.rem(me + k, n), me).start()
        return carry

    atom_copy(lax.rem(me + n // 2, n), me).start()
    lax.fori_loop(1, n // 2, start_atom, 0)
    atom_recv[me] = atom_send[me]

    def take_meta(i, carry):
        src = lax.rem(me + i, n)
        meta_copy(src, src).wait_recv()
        return carry

    lax.fori_loop(1, n, take_meta, 0)
    named = jnp.sum(meta_recv[...], axis=0)
    atoms = gathered.shape[0]
    ids = lines((atoms, 128), 0) + 1
    chosen = jnp.concatenate(
        [(ids == named[r : r + 1]).astype(f32).astype(bf16) for r in range(chunks)], axis=1
    )

    def take_atom(i, carry):
        src = lax.rem(me + i, n)
        atom_copy(src, src).wait_recv()
        return carry

    lax.fori_loop(1, n, take_atom, 0)
    gathered[...] = dot(
        chosen, atom_recv[...].reshape(n * acap, atom_recv.shape[2])
    ).astype(bf16)
    edge_copy.wait()

    def finish(k, carry):
        d = lax.rem(me + k, n)
        meta_copy(d, me).wait_send()
        atom_copy(d, me).wait_send()
        return carry

    lax.fori_loop(1, n, finish, 0)
    for q in spots:
        goal_copy(q, spot).wait_send()
        for h in range(pieces):
            part_copy(h, q, spot).wait_send()
    for z in layers:
        for h in range(pieces):
            plane_copy(h, z, layer).wait_send()
    for g in others:
        low_copy(g, mine).wait_send()
        up_copy(g, mine).wait_send()
        for h in range(pieces):
            pair_copy(h, g, mine).wait_send()


def atom_layers(
    edge_h, gathered_h, feats_h, first_h, second_h, edge_out, atom_h,
    edge, gathered, feats, first, second, atom_out, load_sem, in_sem, out_sem,
):
    loads = [
        pltpu.make_async_copy(src, dst, load_sem.at[i])
        for i, (src, dst) in enumerate(
            [(gathered_h, gathered), (first_h, first), (second_h, second), (feats_h, feats)]
        )
    ]
    share = edge.shape[0] // 4
    strips = [pl.ds(i * share, share) for i in range(4)]
    ins = [
        pltpu.make_async_copy(edge_h.at[at], edge.at[at], in_sem.at[i])
        for i, at in enumerate(strips)
    ]
    outs = [
        pltpu.make_async_copy(edge.at[at], edge_out.at[at], out_sem.at[i])
        for i, at in enumerate(strips)
    ]
    for copy in loads + ins:
        copy.start()
    for arrive, leave in zip(ins, outs):
        arrive.wait()
        leave.start()
    for load in loads:
        load.wait()
    hidden = silu(dot(gathered[...], first[...])).astype(bf16)
    atom_out[...] = (feats[...].astype(f32) + dot(hidden, second[...])).astype(bf16)
    outs.append(pltpu.make_async_copy(atom_out, atom_h, load_sem.at[4]))
    outs[-1].start()
    for leave in outs:
        leave.wait()


def body(
    edge_feats, pre_weight, down_weight, angle_tiles, part_source, part_owner, part_target,
    up_weight, res_first, res_second, edge_slot, slot_owner, slot_atom, atom_feats,
    atom_first, atom_second,
):
    n, groups = lax.axis_size("graph"), lax.axis_size("basis")
    parts, _, block, _ = angle_tiles.shape
    narrow = down_weight.shape[1]
    rows, wide = edge_feats.shape
    nb = rows // block
    slot_count = slot_owner.shape[1]
    cap = max(2, 2 * parts // n)
    acap = -(-max(2, 2 * slot_count // n) // 16) * 16

    seat = -(-cap // 8) * 8
    chunks = n * acap // 128
    meta_rows = -(-chunks // 8) * 8
    pieces = min(2, block // 32)
    inner = 1
    while n % (2 * inner) == 0 and inner * inner < n:
        inner *= 2
    outer = n // inner
    piece = block // 2 // pieces

    half, pair_width = block // 2, 2 * narrow
    dma = pltpu.SemaphoreType.DMA
    vmem = pl.BlockSpec(memory_space=pltpu.VMEM)
    hbm = pl.BlockSpec(memory_space=pl.ANY)
    scratch = [
        pltpu.SMEM((parts,), jnp.int32),
        pltpu.VMEM((1, parts), jnp.int32),
        pltpu.VMEM((1, parts), jnp.int32),
        pltpu.VMEM((1, slot_count), jnp.int32),
        pltpu.VMEM((1, slot_count), jnp.int32),
        pltpu.VMEM((1, rows), jnp.int32),
        pltpu.VMEM(edge_feats.shape, bf16),
        pltpu.VMEM(edge_feats.shape, bf16),
        pltpu.VMEM(pre_weight.shape, bf16),
        pltpu.VMEM(down_weight.shape[::-1], bf16),
        pltpu.VMEM(angle_tiles.shape, bf16),
        pltpu.VMEM((groups,) + up_weight.shape[1:], bf16),
        pltpu.VMEM(res_first.shape, bf16),
        pltpu.VMEM(res_second.shape, bf16),
        pltpu.VMEM((groups, nb, half, pair_width), bf16),
        pltpu.VMEM((groups * nb, 2 * block, pair_width), bf16),
        pltpu.VMEM((parts, half, pair_width), bf16),
        pltpu.VMEM((pieces, inner, outer, cap, piece, pair_width), bf16),
        pltpu.VMEM((pieces, inner, outer, cap, piece, pair_width), bf16),
        pltpu.VMEM((inner, outer, seat, 128), jnp.int32),
        pltpu.VMEM((inner, outer, seat, 128), jnp.int32),
        pltpu.VMEM((n, meta_rows, 128), jnp.int32),
        pltpu.VMEM((n, meta_rows, 128), jnp.int32),
        pltpu.VMEM((1, n * seat), jnp.int32),
        pltpu.SMEM((1, n * seat), jnp.int32),
        pltpu.VMEM((pieces, outer, groups * nb, piece, pair_width), bf16),
        pltpu.VMEM((pieces, outer, groups * nb, piece, pair_width), bf16),
        pltpu.VMEM((pieces, groups, nb * piece, pair_width), bf16),
        pltpu.VMEM((pieces, groups, nb * piece, pair_width), bf16),
        pltpu.VMEM((n * acap, rows), bf16),
        pltpu.VMEM((n, acap, wide), bf16),
        pltpu.VMEM((n, acap, wide), bf16),
        dma((7,)),
        dma((6,)),
        dma((1,)),
        dma((1,)),
    ]
    scratch += [dma((inner,))] * 2 + [dma((n,))] * 2 + [dma((pieces, inner))] * 2
    scratch += [dma((pieces, outer))] * 2 + [dma((n,))] * 2
    scratch += [dma((groups,))] * 4 + [dma((pieces, groups))] * 2
    shapes = (
        jax.ShapeDtypeStruct(edge_feats.shape, bf16),
        jax.ShapeDtypeStruct(atom_feats.shape, bf16),
    )
    edge_update, gathered = pl.pallas_call(
        functools.partial(kernel, n, inner, groups, cap, acap, seat, chunks, nb, block),
        out_shape=shapes,
        in_specs=[hbm] * 13,
        out_specs=(hbm, vmem),
        scratch_shapes=scratch,
        compiler_params=pltpu.CompilerParams(
            collective_id=0, has_side_effects=True, vmem_limit_bytes=62 * 2**20
        ),
    )(
        part_source, part_owner.reshape(1, parts), part_target.reshape(1, parts),
        slot_owner.reshape(1, slot_count), slot_atom, edge_slot,
        edge_feats, pre_weight, down_weight.T,
        angle_tiles, up_weight, res_first, res_second,
    )
    return pl.pallas_call(
        atom_layers,
        out_shape=shapes,
        in_specs=[hbm] * 5,
        out_specs=(hbm, hbm),
        scratch_shapes=[
            pltpu.VMEM(edge_feats.shape, bf16),
            pltpu.VMEM(atom_feats.shape, bf16),
            pltpu.VMEM(atom_feats.shape, bf16),
            pltpu.VMEM(atom_first.shape, bf16),
            pltpu.VMEM(atom_second.shape, bf16),
            pltpu.VMEM(atom_feats.shape, bf16),
            dma((5,)),
            dma((4,)),
            dma((4,)),
        ],
        compiler_params=pltpu.CompilerParams(vmem_limit_bytes=62 * 2**20),
    )(edge_update, gathered, atom_feats, atom_first, atom_second)


def solution(mesh):
    rows = P(("graph", "basis"), None)
    in_specs = (
        rows,
        P(),
        P(),
        P("graph", "basis", None, None),
        P("graph"),
        P("graph", None),
        P("graph"),
        P("basis", None, None),
        P(),
        P(),
        rows,
        P(("graph", "basis"), None, None),
        rows,
        rows,
        P(),
        P(),
    )
    return jax.shard_map(
        body, mesh=mesh, in_specs=in_specs, out_specs=(rows, rows), check_vma=False
    )
```
